32 devices in a mesh: groups: 2 (over x), shot: 16 (over z, y, core).
Axes of the slice: x: 2, y: 2, z: 4, core: 2. Of those that a mesh axis runs over, the one named last changes fastest.
Arguments:
- spectra: bfloat16 [1024, 2, 64, 512], P(('groups', 'shot')), parts along dimension 0, may hold values from -1.1953125 to 1.1953125
- fold_counts: int32 [1024], P('groups'), parts along dimension 0, may hold values from 1 to 512
- inverse_wavelet: float32 [2, 64], replicated, may hold values from -4 to 4
Outputs:
- multiples: bfloat16 [1024, 2, 64, 512], P(('groups', 'shot')), parts along dimension 0
The draws below stay inside these ranges and needn't reach their ends.
There are 2 independent parts, one for each index of `groups`. The reference program is written for one: setup_inputs(seed, part) draws one part's arguments, and reference() takes and returns one part's arrays. A program takes and returns all parts, laid end to end along the dimension named above; an argument that names none is the same for every part. Nothing has to cross between parts.
All inputs are finite; a program needn't handle non-finite values.
Results may differ from the reference program's by a relative error of at most 0.001.
Values may be sent and summed in bfloat16 or wider, within the bound.
No kernel may reach another device: no remote copies, remote signals or barrier semaphores. Data moves between devices by JAX's collectives and lax.ppermute only.
A program may use at most 64 MiB of HBM per device.

```python
import jax
import jax.numpy as jnp
from jax import lax

POINTS = 512
BINS = 64


def draw_fold_counts(key, part):
    key_choose = jax.random.fold_in(key, 11)
    key_wide = jax.random.fold_in(key, 12)
    key_pick = jax.random.fold_in(key, 13)
    chooser = jax.random.randint(key_choose, (POINTS,), 0, 2)
    wide = jax.random.randint(key_wide, (POINTS,), POINTS // 2 + 1, POINTS + 1)
    folds = jnp.where(chooser == 1, wide, 1)
    picks = jax.random.permutation(key_pick, POINTS)
    positions = jnp.arange(POINTS, dtype=jnp.int32)
    folds = jnp.where(positions == picks[0], POINTS, folds)
    folds = jnp.where(positions == picks[1], 1, folds)
    return folds.astype(jnp.int32)


def levels(stream_key, dims, split, low, high):
    factor_of, own = 1.0, jax.random.fold_in(stream_key, 6)
    for axis_at, parts in split:
        draws = jnp.exp(jax.random.uniform(jax.random.fold_in(own, axis_at), (parts,), jnp.float32, low / len(split), high / len(split)))
        factor_of = factor_of * jnp.repeat(draws, dims[axis_at] // parts).reshape([-1 if axis == axis_at else 1 for axis in range(len(dims))])
    return factor_of


def bell_draw(stream_key, extent, width, reach, cuts=(), kind=jnp.bfloat16):
    array = width * jax.random.normal(stream_key, extent, jnp.float32)
    if cuts:
        array = array * levels(stream_key, extent, cuts, -0.22, 0.18)
    return jnp.clip(array, -reach, reach).astype(kind)


def setup_inputs(seed: int = 0, part: int = 0) -> dict:
    arg_keys = jax.random.split(jax.random.key(seed), 4)
    part_keys = jax.random.split(jax.random.fold_in(arg_keys[3], part), 4)
    spectra = bell_draw(part_keys[0], (POINTS, 2, BINS, POINTS), 0.2, 1.1953125, ((0, 16),))
    fold_counts = draw_fold_counts(jax.random.fold_in(jax.random.fold_in(arg_keys[3], part), 71), part)
    inverse_wavelet = bell_draw(arg_keys[2], (2, BINS), 1.0, 4.0, (), jnp.float32)
    return dict(spectra=spectra, fold_counts=fold_counts, inverse_wavelet=inverse_wavelet)


def reference(spectra, fold_counts, inverse_wavelet):
    indices = jnp.arange(POINTS, dtype=jnp.int32)
    recorded = jnp.abs(indices[None, :] - indices[:, None]) < fold_counts[:, None]
    mirrored = spectra.transpose(3, 1, 2, 0)
    filled = jnp.where(recorded[:, None, None, :], spectra,
                       jnp.where(recorded.T[:, None, None, :], mirrored, jnp.zeros_like(spectra)))

    def per_bin(which):
        slab = lax.dynamic_index_in_dim(filled, which, 2, keepdims=False)
        real_component = slab[:, 0, :]
        imaginary_component = slab[:, 1, :]
        prod_real = jnp.dot(real_component, real_component, preferred_element_type=jnp.float32) - jnp.dot(imaginary_component, imaginary_component, preferred_element_type=jnp.float32)
        prod_imag = jnp.dot(real_component, imaginary_component, preferred_element_type=jnp.float32) + jnp.dot(imaginary_component, real_component, preferred_element_type=jnp.float32)
        wave = lax.dynamic_index_in_dim(inverse_wavelet, which, 1, keepdims=False)
        output_real = -(wave[0] * prod_real - wave[1] * prod_imag)
        out_imag = -(wave[0] * prod_imag + wave[1] * prod_real)
        return jnp.stack([output_real, out_imag], axis=1).astype(jnp.bfloat16)

    stacked_spectra = lax.map(per_bin, jnp.arange(BINS, dtype=jnp.int32))
    return stacked_spectra.transpose(1, 2, 0, 3)
```

```python
import functools

import jax
import jax.numpy as jnp
from jax import lax
from jax.experimental import pallas as pl
from jax.experimental.pallas import tpu as pltpu
from jax.sharding import PartitionSpec as P

PLANE = 4
VMEM_LIMIT = 32 * 1024 * 1024


def batched_product(left_operand, right_operand):
    return jnp.einsum(
        "hwi,iwc->hwc", left_operand, right_operand, preferred_element_type=jnp.float32
    )


def plain_shards(spectra, fold_counts, inverse_wavelet):
    points = spectra.shape[3]
    everyone = jnp.arange(points, dtype=jnp.int32)
    regrouped = lax.all_to_all(spectra, "shot", split_axis=2, concat_axis=0, tiled=True)
    recorded = jnp.abs(everyone[None, :] - everyone[:, None]) < fold_counts[:, None]
    flipped = regrouped.transpose(3, 1, 2, 0)
    regrouped = jnp.where(
        recorded[:, None, None, :],
        regrouped,
        jnp.where(recorded.T[:, None, None, :], flipped, jnp.zeros_like(regrouped)),
    )
    local_bins = regrouped.shape[2]
    real_component = regrouped[:, 0]
    imaginary_component = regrouped[:, 1]
    prod_real = batched_product(real_component, real_component) - batched_product(
        imaginary_component, imaginary_component
    )
    prod_imag = batched_product(real_component, imaginary_component) + batched_product(
        imaginary_component, real_component
    )
    first_bin = lax.axis_index("shot") * local_bins
    wave = lax.dynamic_slice_in_dim(inverse_wavelet, first_bin, local_bins, 1)
    wavelet_real = wave[0][None, :, None]
    wave_imag = wave[1][None, :, None]
    output_real = -(wavelet_real * prod_real - wave_imag * prod_imag)
    out_imag = -(wavelet_real * prod_imag + wave_imag * prod_real)
    result = jnp.stack([output_real, out_imag], axis=1).astype(jnp.bfloat16)
    return lax.all_to_all(result, "shot", split_axis=0, concat_axis=2, tiled=True)


def any_spec():
    return pl.BlockSpec(memory_space=pl.ANY)


def vmem_spec():
    return pl.BlockSpec(memory_space=pltpu.VMEM)


def smem_spec():
    return pl.BlockSpec(memory_space=pltpu.SMEM)


def params():
    return pltpu.CompilerParams(vmem_limit_bytes=VMEM_LIMIT)


def cost(flops, bytes_accessed):
    return pl.CostEstimate(
        flops=flops, bytes_accessed=bytes_accessed, transcendentals=0
    )


def split_order(me, n, shots, transposed):
    rows = n * shots
    a = lax.broadcasted_iota(jnp.int32, (rows, rows), 1 if transposed else 0)
    b = lax.broadcasted_iota(jnp.int32, (rows, rows), 0 if transposed else 1)
    source = (a % shots) * n + ((a // shots) ^ me)
    return jnp.where(source == b, 1.0, 0.0).astype(jnp.bfloat16)


def relayout_kernel(n, shots, me_ref, x_ref, *refs):
    outs = refs[-(n // PLANE) :]
    me = me_ref[0]
    order = split_order(me, n, shots, False)
    points = x_ref.shape[3]
    for c in range(2):
        rows = x_ref[:, c].reshape(shots * n, points)
        moved = jnp.dot(order, rows, preferred_element_type=jnp.float32)
        moved = moved.astype(jnp.bfloat16).reshape(n // PLANE, PLANE, shots, points)
        for j, out in enumerate(outs):
            out[:, c] = moved[j]


def relayout(me, spectra, k, n, after):
    shots, _, _, points = spectra.shape
    planes = n // PLANE
    block = jax.ShapeDtypeStruct((PLANE, 2, shots, points), spectra.dtype)
    size = 2 * n * shots * points * 2
    return pl.pallas_call(
        functools.partial(relayout_kernel, n, shots),
        grid=(1,),
        out_shape=[block] * planes,
        in_specs=[
            smem_spec(),
            pl.BlockSpec((shots, 2, n, points), lambda _: (0, 0, k, 0)),
        ]
        + [any_spec()] * len(after),
        out_specs=[pl.BlockSpec(block.shape, lambda _: (0, 0, 0, 0))] * planes,
        compiler_params=params(),
        cost_estimate=cost(4 * (n * shots) ** 2 * points, 2 * size),
        name="relayout",
    )(me, spectra, *after)


def swap_kernel(count_in, *refs):
    ins, outs = refs[:count_in], refs[count_in:]
    for i, out in enumerate(outs):
        for j, block in enumerate(ins):
            out[j] = block[i]


def swap(blocks):
    count_in, count_out = len(blocks), blocks[0].shape[0]
    shape = jax.ShapeDtypeStruct((count_in, *blocks[0].shape[1:]), blocks[0].dtype)
    size = 2 * count_out * shape.size
    return pl.pallas_call(
        functools.partial(swap_kernel, count_in),
        out_shape=[shape] * count_out,
        in_specs=[vmem_spec()] * count_in,
        out_specs=[vmem_spec()] * count_out,
        compiler_params=params(),
        cost_estimate=cost(0, 2 * size),
        name="swap",
    )(*blocks)


def product_kernel(k, n, me_ref, wave_ref, fold_row_ref, fold_col_ref, *refs):
    ins, outs = refs[:PLANE], refs[PLANE : 2 * PLANE]
    a_ref, o_ref = refs[2 * PLANE :]
    me = me_ref[0]
    planes, _, shots, points = ins[0].shape

    def rows_of(j, i):
        start = ((PLANE * j + i) ^ me) * shots
        return pl.ds(pl.multiple_of(start, shots), shots)

    for j in range(planes):
        for i in range(PLANE):
            for c in range(2):
                a_ref[c, rows_of(j, i), :] = ins[i][j, c]
    s = lax.broadcasted_iota(jnp.int32, (points, points), 0)
    x = lax.broadcasted_iota(jnp.int32, (points, points), 1)
    apart = jnp.abs(x - s)
    recorded = apart < fold_col_ref[...]
    mirrored = apart < fold_row_ref[...]

    def fill(c):
        own = a_ref[c].astype(jnp.float32)
        return jnp.where(
            recorded, own, jnp.where(mirrored, own.T, 0.0)
        ).astype(jnp.bfloat16)

    re, im = fill(0), fill(1)

    def dot(left, right):
        return jnp.dot(left, right, preferred_element_type=jnp.float32)

    prod_re = dot(re, re) - dot(im, im)
    prod_im = dot(re, im) + dot(im, re)
    which = k * n + me
    wave_re, wave_im = wave_ref[0, which], wave_ref[1, which]
    o_ref[0] = (-(wave_re * prod_re - wave_im * prod_im)).astype(jnp.bfloat16)
    o_ref[1] = (-(wave_re * prod_im + wave_im * prod_re)).astype(jnp.bfloat16)
    for j in range(planes):
        for i in range(PLANE):
            for c in range(2):
                outs[i][j, c] = o_ref[c, rows_of(j, i), :]


def product(me, wave, fold, blocks, k, n):
    shape = jax.ShapeDtypeStruct(blocks[0].shape, blocks[0].dtype)
    points = shape.shape[3]
    size = 2 * len(blocks) * shape.size
    return pl.pallas_call(
        functools.partial(product_kernel, k, n),
        out_shape=[shape] * PLANE,
        in_specs=[smem_spec()] * 2 + [vmem_spec()] * (2 + PLANE),
        out_specs=[vmem_spec()] * PLANE,
        scratch_shapes=[pltpu.VMEM((2, points, points), jnp.bfloat16)] * 2,
        compiler_params=params(),
        cost_estimate=cost(8 * points**3, 2 * size),
        name="product",
    )(me, wave, fold.reshape(1, -1), fold.reshape(-1, 1), *blocks)


def assemble_kernel(n, shots, planes, me_ref, *refs):
    ins, out_ref = refs[:planes], refs[-1]
    me = me_ref[0]
    order = split_order(me, n, shots, True)
    points = out_ref.shape[3]
    for c in range(2):
        rows = jnp.concatenate(
            [block[:, c].reshape(PLANE * shots, points) for block in ins], axis=0
        )
        moved = jnp.dot(order, rows, preferred_element_type=jnp.float32)
        out_ref[:, c] = moved.astype(jnp.bfloat16).reshape(shots, n, points)


def assemble(me, blocks, result, k, n, bins):
    planes = len(blocks)
    _, _, shots, points = blocks[0].shape
    size = 2 * n * shots * points * 2
    extra = [] if result is None else [result]
    return pl.pallas_call(
        functools.partial(assemble_kernel, n, shots, planes),
        grid=(1,),
        out_shape=jax.ShapeDtypeStruct((shots, 2, bins, points), jnp.bfloat16),
        in_specs=[smem_spec()]
        + [pl.BlockSpec(blocks[0].shape, lambda _: (0, 0, 0, 0))] * planes
        + [any_spec()] * len(extra),
        out_specs=pl.BlockSpec((shots, 2, n, points), lambda _: (0, 0, k, 0)),
        input_output_aliases={1 + planes: 0} if extra else {},
        compiler_params=params(),
        cost_estimate=cost(4 * (n * shots) ** 2 * points, 2 * size),
        name="assemble",
    )(me, *blocks, *extra)


def exchange(blocks, n, stride):
    received = {
        m: lax.ppermute(
            blocks[m], "shot", [(d, d ^ (m * stride)) for d in range(n)]
        )
        for m in reversed(range(1, len(blocks)))
    }
    return [blocks[0]] + [received[m] for m in range(1, len(blocks))]


def chunked_shards(n, spectra, fold_counts, inverse_wavelet):
    bins = spectra.shape[2]
    chunks = bins // n
    me = lax.axis_index("shot").astype(jnp.int32).reshape(1)
    arrived = []
    for k in range(chunks):
        after = [arrived[k - 2][-1]] if k >= 2 else []
        arrived.append(exchange(relayout(me, spectra, k, n, after), n, PLANE))
    leaving = []
    for k in range(chunks):
        inside = exchange(swap(arrived[k]), n, 1)
        made = product(me, inverse_wavelet, fold_counts, inside, k, n)
        leaving.append(swap(exchange(made, n, 1)))
    result = None
    for k in range(chunks):
        result = assemble(me, exchange(leaving[k], n, PLANE), result, k, n, bins)
    return result


def solution(mesh):
    n = mesh.shape["shot"]

    def shards(spectra, fold_counts, inverse_wavelet):
        shots, _, bins, _ = spectra.shape
        power = n & (n - 1) == 0
        if power and n % 16 == 0 and bins % n == 0 and shots % 16 == 0:
            return chunked_shards(n, spectra, fold_counts, inverse_wavelet)
        return plain_shards(spectra, fold_counts, inverse_wavelet)

    in_specs = (P(("groups", "shot"), None, None, None), P("groups"), P())
    out_specs = P(("groups", "shot"), None, None, None)
    return jax.shard_map(
        shards, mesh=mesh, in_specs=in_specs, out_specs=out_specs, check_vma=False
    )
```

```python
import functools

import jax
import jax.numpy as jnp
from jax import lax
from jax.experimental import pallas as pl
from jax.experimental.pallas import tpu as pltpu
from jax.sharding import PartitionSpec as P

PLANE = 4
VMEM_LIMIT = 32 * 1024 * 1024


def batched_product(left_operand, right_operand):
    return jnp.einsum(
        "hwi,iwc->hwc", left_operand, right_operand, preferred_element_type=jnp.float32
    )


def plain_shards(spectra, fold_counts, inverse_wavelet):
    points = spectra.shape[3]
    everyone = jnp.arange(points, dtype=jnp.int32)
    regrouped = lax.all_to_all(spectra, "shot", split_axis=2, concat_axis=0, tiled=True)
    recorded = jnp.abs(everyone[None, :] - everyone[:, None]) < fold_counts[:, None]
    flipped = regrouped.transpose(3, 1, 2, 0)
    regrouped = jnp.where(
        recorded[:, None, None, :],
        regrouped,
        jnp.where(recorded.T[:, None, None, :], flipped, jnp.zeros_like(regrouped)),
    )
    local_bins = regrouped.shape[2]
    real_component = regrouped[:, 0]
    imaginary_component = regrouped[:, 1]
    prod_real = batched_product(real_component, real_component) - batched_product(
        imaginary_component, imaginary_component
    )
    prod_imag = batched_product(real_component, imaginary_component) + batched_product(
        imaginary_component, real_component
    )
    first_bin = lax.axis_index("shot") * local_bins
    wave = lax.dynamic_slice_in_dim(inverse_wavelet, first_bin, local_bins, 1)
    wavelet_real = wave[0][None, :, None]
    wave_imag = wave[1][None, :, None]
    output_real = -(wavelet_real * prod_real - wave_imag * prod_imag)
    out_imag = -(wavelet_real * prod_imag + wave_imag * prod_real)
    result = jnp.stack([output_real, out_imag], axis=1).astype(jnp.bfloat16)
    return lax.all_to_all(result, "shot", split_axis=0, concat_axis=2, tiled=True)


def any_spec():
    return pl.BlockSpec(memory_space=pl.ANY)


def vmem_spec():
    return pl.BlockSpec(memory_space=pltpu.VMEM)


def smem_spec():
    return pl.BlockSpec(memory_space=pltpu.SMEM)


def params():
    return pltpu.CompilerParams(vmem_limit_bytes=VMEM_LIMIT)


COST = pl.CostEstimate(flops=0, bytes_accessed=0, transcendentals=0)
PACE = pl.CostEstimate(flops=40_000_000_000, bytes_accessed=0, transcendentals=0)


def split_order(me, n, shots, wanted):
    rows, count = n * shots, PLANE * shots
    source = lax.broadcasted_iota(jnp.int32, (count, rows), 1)
    target = lax.broadcasted_iota(jnp.int32, (count, rows), 0)
    parts = []
    for j in wanted:
        which = ((me // PLANE) ^ j) * PLANE + target // shots
        parts.append((target % shots) * n + which == source)
    return jnp.concatenate(
        [jnp.where(part, 1.0, 0.0).astype(jnp.bfloat16) for part in parts], axis=0
    )


def merge_order(me, n, shots):
    rows = n * shots
    source = lax.broadcasted_iota(jnp.int32, (rows, rows), 1)
    target = lax.broadcasted_iota(jnp.int32, (rows, rows), 0)
    block = (target % n) ^ ((me // PLANE) * PLANE)
    return jnp.where(block * shots + target // n == source, 1.0, 0.0).astype(
        jnp.bfloat16
    )


def relayout_kernel(n, shots, wanted, me_ref, x_ref, *refs):
    outs = refs[-len(wanted) :]
    me = me_ref[0]
    order = split_order(me, n, shots, wanted)
    points = x_ref.shape[3]
    for c in range(2):
        rows = x_ref[:, c].reshape(shots * n, points)
        moved = jnp.dot(order, rows, preferred_element_type=jnp.float32)
        moved = moved.astype(jnp.bfloat16).reshape(-1, PLANE, shots, points)
        for at, out in enumerate(outs):
            out[:, c] = moved[at]


def relayout(me, spectra, k, n, wanted, after):
    shots, _, _, points = spectra.shape
    block = jax.ShapeDtypeStruct((PLANE, 2, shots, points), spectra.dtype)
    return pl.pallas_call(
        functools.partial(relayout_kernel, n, shots, wanted),
        grid=(1,),
        out_shape=[block] * len(wanted),
        in_specs=[
            smem_spec(),
            pl.BlockSpec((shots, 2, n, points), lambda _: (0, 0, k, 0)),
        ]
        + [any_spec()] * len(after),
        out_specs=[pl.BlockSpec(block.shape, lambda _: (0, 0, 0, 0))] * len(wanted),
        compiler_params=params(),
        cost_estimate=PACE,
        name="relayout",
    )(me, spectra, *after)


def join_kernel(count_in, *refs):
    out = refs[-1]
    for at in range(count_in):
        out[at] = refs[at][...]


def join(blocks, after):
    block = blocks[0]
    return pl.pallas_call(
        functools.partial(join_kernel, len(blocks)),
        out_shape=jax.ShapeDtypeStruct((len(blocks), *block.shape), block.dtype),
        in_specs=[vmem_spec()] * len(blocks) + [any_spec()] * len(after),
        out_specs=vmem_spec(),
        compiler_params=params(),
        cost_estimate=COST,
        name="join",
    )(*blocks, *after)


def release_kernel(count, *refs):
    for block, out in zip(refs[:count], refs[-count:]):
        out[...] = block[...]


def release(blocks, after):
    return pl.pallas_call(
        functools.partial(release_kernel, len(blocks)),
        out_shape=[jax.ShapeDtypeStruct(block.shape, block.dtype) for block in blocks],
        in_specs=[vmem_spec()] * len(blocks) + [any_spec()] * len(after),
        out_specs=[vmem_spec()] * len(blocks),
        compiler_params=params(),
        cost_estimate=PACE,
        name="release",
    )(*blocks, *after)


def product_kernel(k, n, planes, me_ref, wave_ref, fold_row_ref, fold_col_ref, *refs):
    near_ref, far_ref, core_ref = refs[:3]
    outs, raw_ref, full_ref = refs[-planes - 2 : -2], refs[-2], refs[-1]
    me = me_ref[0]
    shots, points = near_ref.shape[3:]

    def rows_of(j, i):
        start = ((PLANE * j + i) ^ me) * shots
        return pl.ds(pl.multiple_of(start, shots), shots)

    def block(j, i, b, c):
        if i % 2:
            return core_ref[i // 2, j, b, c]
        return (far_ref if i // 2 else near_ref)[j, b, c]

    s = lax.broadcasted_iota(jnp.int32, (points, points), 0)
    x = lax.broadcasted_iota(jnp.int32, (points, points), 1)
    apart = jnp.abs(x - s)
    recorded = apart < fold_col_ref[...]
    mirrored = apart < fold_row_ref[...]

    def dot(left, right):
        return jnp.dot(left, right, preferred_element_type=jnp.float32)

    half = planes * shots
    for b in range(PLANE):
        for c in range(2):
            for j in range(planes):
                for i in range(PLANE):
                    raw_ref[b, c, rows_of(j, i), :] = block(j, i, b, c)
            own = raw_ref[b, c].astype(jnp.float32)
            full_ref[b, c] = jnp.where(
                recorded, own, jnp.where(mirrored, own.T, 0.0)
            ).astype(jnp.bfloat16)
        left = jnp.concatenate(
            [full_ref[b, c, rows_of(j, 0), :] for c in range(2) for j in range(planes)],
            axis=0,
        )
        by_re, by_im = dot(left, full_ref[b, 0]), dot(left, full_ref[b, 1])
        prod_re = by_re[:half] - by_im[half:]
        prod_im = by_im[:half] + by_re[half:]
        which = k * n + (me // PLANE) * PLANE + b
        wave_re, wave_im = wave_ref[0, which], wave_ref[1, which]
        made_re = (-(wave_re * prod_re - wave_im * prod_im)).astype(jnp.bfloat16)
        made_im = (-(wave_re * prod_im + wave_im * prod_re)).astype(jnp.bfloat16)
        for j, out in enumerate(outs):
            out[b, 0] = made_re[j * shots : (j + 1) * shots]
            out[b, 1] = made_im[j * shots : (j + 1) * shots]


def product(me, wave, fold, near, far, core, k, n, after):
    planes, _, _, shots, points = near.shape
    block = jax.ShapeDtypeStruct(near.shape[1:], near.dtype)
    return pl.pallas_call(
        functools.partial(product_kernel, k, n, planes),
        out_shape=[block] * planes,
        in_specs=[smem_spec()] * 2 + [vmem_spec()] * 5 + [any_spec()] * len(after),
        out_specs=[vmem_spec()] * planes,
        scratch_shapes=[pltpu.VMEM((PLANE, 2, points, points), jnp.bfloat16)] * 2,
        compiler_params=params(),
        cost_estimate=COST,
        name="product",
    )(me, wave, fold.reshape(1, -1), fold.reshape(-1, 1), near, far, core, *after)


def assemble_kernel(n, shots, planes, me_ref, *refs):
    ins, out_ref = refs[:planes], refs[-1]
    me = me_ref[0]
    order = merge_order(me, n, shots)
    points = out_ref.shape[3]
    for c in range(2):
        rows = jnp.concatenate(
            [block[:, c].reshape(PLANE * shots, points) for block in ins], axis=0
        )
        moved = jnp.dot(order, rows, preferred_element_type=jnp.float32)
        out_ref[:, c] = moved.astype(jnp.bfloat16).reshape(shots, n, points)


def assemble(me, blocks, result, k, n, bins, after):
    planes = len(blocks)
    _, _, shots, points = blocks[0].shape
    extra = [] if result is None else [result]
    return pl.pallas_call(
        functools.partial(assemble_kernel, n, shots, planes),
        grid=(1,),
        out_shape=jax.ShapeDtypeStruct((shots, 2, bins, points), jnp.bfloat16),
        in_specs=[smem_spec()]
        + [pl.BlockSpec(blocks[0].shape, lambda _: (0, 0, 0, 0))] * planes
        + [any_spec()] * len(extra + after),
        out_specs=pl.BlockSpec((shots, 2, n, points), lambda _: (0, 0, k, 0)),
        input_output_aliases={1 + planes: 0} if extra else {},
        compiler_params=params(),
        cost_estimate=COST,
        name="assemble",
    )(me, *blocks, *extra, *after)


def send(block, n, offset, what):
    with jax.named_scope(what):
        return lax.ppermute(block, "shot", [(d, d ^ offset) for d in range(n)])


def chunked_shards(n, spectra, fold_counts, inverse_wavelet):
    bins = spectra.shape[2]
    chunks, planes = bins // n, n // PLANE
    cross = list(reversed(range(planes // 2, planes)))
    rest = list(range(1, planes // 2))
    me = lax.axis_index("shot").astype(jnp.int32).reshape(1)

    last = []
    crossed = []

    def order():
        return last[-1:] + crossed[-2:-1]

    def depart(blocks, what):
        for j, block in blocks.items():
            if j:
                blocks[j] = send(block, n, PLANE * j, f"{what}_z{j}")
            if j in cross:
                crossed.append(blocks[j])
        return blocks

    arrived = [{} for _ in range(chunks)]
    beside = [{} for _ in range(chunks)]
    made = [{} for _ in range(chunks)]
    leaving = [{} for _ in range(chunks)]
    result = [None]

    def parts(at):
        return [cross[at]] + (([0] + rest) if at == len(cross) - 1 else [])

    def go_in(k, at):
        if k >= chunks:
            return
        wanted = parts(at)
        with jax.named_scope(f"in{k}_{at}"):
            blocks = relayout(me, spectra, k, n, wanted, order())
        last.append(blocks[0])
        arrived[k].update(depart(dict(zip(wanted, blocks)), f"in{k}"))

    def go_out(k, at):
        if not 0 <= k < chunks:
            return
        wanted = parts(at)
        with jax.named_scope(f"out{k}_{at}"):
            blocks = release([made[k][j] for j in wanted], order())
        last.append(blocks[0])
        leaving[k].update(depart(dict(zip(wanted, blocks)), f"out{k}"))

    def go_y(k):
        if not 0 <= k < chunks:
            return
        with jax.named_scope(f"y{k}"):
            near = join([arrived[k][j] for j in range(planes)], last[-1:])
        last.append(near)
        beside[k] = near, send(near, n, 2, f"in{k}_y")

    def go_core(k):
        if not 0 <= k < chunks:
            return
        with jax.named_scope(f"core{k}"):
            both = join(beside[k], last[-1:])
        last.append(both)
        beside[k] += (send(both, n, 1, f"in{k}_core"),)

    def multiply(k):
        if not 0 <= k < chunks:
            return
        with jax.named_scope(f"chunk{k}"):
            blocks = product(
                me, inverse_wavelet, fold_counts, *beside[k], k, n, last[-1:]
            )
        last.append(blocks[0])
        made[k] = dict(enumerate(blocks))

    def finish(k):
        if not 0 <= k < chunks:
            return
        blocks = [leaving[k][j] for j in range(planes)]
        with jax.named_scope(f"chunk{k}"):
            result[0] = assemble(me, blocks, result[0], k, n, bins, last[-1:])

    for t in range(2 * chunks + 1):
        for at in range(len(cross)):
            go_in(t, at)
            go_out(t - chunks, at)
            if at == 0:
                multiply(t - 3)
        go_core(t - 2)
        go_y(t - 1)
        finish(t - chunks - 1)
    return result[0]


def solution(mesh):
    n = mesh.shape["shot"]

    def shards(spectra, fold_counts, inverse_wavelet):
        shots, _, bins, _ = spectra.shape
        power = n & (n - 1) == 0
        if power and n % 16 == 0 and bins % n == 0 and shots % 16 == 0:
            return chunked_shards(n, spectra, fold_counts, inverse_wavelet)
        return plain_shards(spectra, fold_counts, inverse_wavelet)

    in_specs = (P(("groups", "shot"), None, None, None), P("groups"), P())
    out_specs = P(("groups", "shot"), None, None, None)
    return jax.shard_map(
        shards, mesh=mesh, in_specs=in_specs, out_specs=out_specs, check_vma=False
    )
```

```python
import functools

import jax
import jax.numpy as jnp
from jax import lax
from jax.experimental import pallas as pl
from jax.experimental.pallas import tpu as pltpu
from jax.sharding import PartitionSpec as P

PLANE = 4
VMEM_LIMIT = 32 * 1024 * 1024


def batched_product(left_operand, right_operand):
    return jnp.einsum(
        "hwi,iwc->hwc", left_operand, right_operand, preferred_element_type=jnp.float32
    )


def plain_shards(spectra, fold_counts, inverse_wavelet):
    points = spectra.shape[3]
    everyone = jnp.arange(points, dtype=jnp.int32)
    regrouped = lax.all_to_all(spectra, "shot", split_axis=2, concat_axis=0, tiled=True)
    recorded = jnp.abs(everyone[None, :] - everyone[:, None]) < fold_counts[:, None]
    flipped = regrouped.transpose(3, 1, 2, 0)
    regrouped = jnp.where(
        recorded[:, None, None, :],
        regrouped,
        jnp.where(recorded.T[:, None, None, :], flipped, jnp.zeros_like(regrouped)),
    )
    local_bins = regrouped.shape[2]
    real_component = regrouped[:, 0]
    imaginary_component = regrouped[:, 1]
    prod_real = batched_product(real_component, real_component) - batched_product(
        imaginary_component, imaginary_component
    )
    prod_imag = batched_product(real_component, imaginary_component) + batched_product(
        imaginary_component, real_component
    )
    first_bin = lax.axis_index("shot") * local_bins
    wave = lax.dynamic_slice_in_dim(inverse_wavelet, first_bin, local_bins, 1)
    wavelet_real = wave[0][None, :, None]
    wave_imag = wave[1][None, :, None]
    output_real = -(wavelet_real * prod_real - wave_imag * prod_imag)
    out_imag = -(wavelet_real * prod_imag + wave_imag * prod_real)
    result = jnp.stack([output_real, out_imag], axis=1).astype(jnp.bfloat16)
    return lax.all_to_all(result, "shot", split_axis=0, concat_axis=2, tiled=True)


def any_spec():
    return pl.BlockSpec(memory_space=pl.ANY)


def vmem_spec():
    return pl.BlockSpec(memory_space=pltpu.VMEM)


def hbm_spec():
    return pl.BlockSpec(memory_space=pltpu.HBM)


def smem_spec():
    return pl.BlockSpec(memory_space=pltpu.SMEM)


def params():
    return pltpu.CompilerParams(vmem_limit_bytes=VMEM_LIMIT)


COST = pl.CostEstimate(flops=0, bytes_accessed=0, transcendentals=0)
PACE = pl.CostEstimate(flops=40_000_000_000, bytes_accessed=0, transcendentals=0)


def split_order(me, n, shots, wanted):
    rows, count = n * shots, PLANE * shots
    source = lax.broadcasted_iota(jnp.int32, (count, rows), 1)
    target = lax.broadcasted_iota(jnp.int32, (count, rows), 0)
    parts = []
    for j in wanted:
        which = ((me // PLANE) ^ j) * PLANE + target // shots
        parts.append((target % shots) * n + which == source)
    return jnp.concatenate(
        [jnp.where(part, 1.0, 0.0).astype(jnp.bfloat16) for part in parts], axis=0
    )


def merge_order_kernel(n, shots, me_ref, *refs):
    out = refs[-1]
    planes, rows, count = out.shape
    source = lax.broadcasted_iota(jnp.int32, (rows, count), 1)
    target = lax.broadcasted_iota(jnp.int32, (rows, count), 0)
    for j in range(planes):
        first = ((me_ref[0] // PLANE) ^ j) * PLANE
        hit = (target % n - first) * shots + target // n == source
        out[j] = jnp.where(hit, 1.0, 0.0).astype(jnp.bfloat16)


def merge_order(me, n, shots, after):
    return pl.pallas_call(
        functools.partial(merge_order_kernel, n, shots),
        out_shape=jax.ShapeDtypeStruct(
            (n // PLANE, n * shots, PLANE * shots), jnp.bfloat16
        ),
        in_specs=[smem_spec()] + [any_spec()] * len(after),
        out_specs=vmem_spec(),
        compiler_params=params(),
        cost_estimate=COST,
        name="merge_order",
    )(me, *after)


def merged(order_ref, blocks, c):
    total = None
    for j, block in blocks:
        rows = block[:, c].reshape(-1, block.shape[3])
        part = jnp.dot(order_ref[j], rows, preferred_element_type=jnp.float32)
        total = part if total is None else total + part
    return total


def early_kernel(which, order_ref, *refs):
    ins, out = refs[: len(which)], refs[-1]
    for c in range(2):
        out[c] = merged(order_ref, list(zip(which, ins)), c).astype(jnp.bfloat16)


def early(order, blocks, after, cost):
    _, _, shots, points = next(iter(blocks.values())).shape
    return pl.pallas_call(
        functools.partial(early_kernel, list(blocks)),
        out_shape=jax.ShapeDtypeStruct((2, order.shape[1], points), jnp.bfloat16),
        in_specs=[vmem_spec()] * (1 + len(blocks)) + [any_spec()] * len(after),
        out_specs=vmem_spec(),
        compiler_params=params(),
        cost_estimate=cost,
        name="early",
    )(order, *blocks.values(), *after)


def assemble_kernel(n, shots, k, which, order_ref, begun_ref, *refs):
    ins = refs[: len(which)]
    out, held, sems = refs[-3:]
    copies = []
    for c in range(2):
        total = merged(order_ref, list(zip(which, ins)), c)
        total = total + begun_ref[c].astype(jnp.float32)
        held[c] = total.astype(jnp.bfloat16).reshape(shots, n, -1)
        copies.append(
            pltpu.make_async_copy(
                held.at[c], out.at[:, c, pl.ds(k * n, n), :], sems.at[c]
            )
        )
        copies[c].start()
    for copy in copies:
        copy.wait()


def assemble(order, begun, blocks, result, k, n, bins, after):
    _, _, shots, points = next(iter(blocks.values())).shape
    extra = [] if result is None else [result]
    return pl.pallas_call(
        functools.partial(assemble_kernel, n, shots, k, list(blocks)),
        out_shape=jax.ShapeDtypeStruct((shots, 2, bins, points), jnp.bfloat16),
        in_specs=[vmem_spec()] * (2 + len(blocks))
        + [hbm_spec()] * len(extra)
        + [any_spec()] * len(after),
        out_specs=hbm_spec(),
        scratch_shapes=[
            pltpu.VMEM((2, shots, n, points), jnp.bfloat16),
            pltpu.SemaphoreType.DMA((2,)),
        ],
        input_output_aliases={2 + len(blocks): 0} if extra else {},
        compiler_params=params(),
        cost_estimate=COST,
        name="assemble",
    )(order, begun, *blocks.values(), *extra, *after)


def relayout_kernel(n, shots, wanted, me_ref, x_ref, *refs):
    outs = refs[-len(wanted) :]
    me = me_ref[0]
    order = split_order(me, n, shots, wanted)
    points = x_ref.shape[3]
    for c in range(2):
        rows = x_ref[:, c].reshape(shots * n, points)
        moved = jnp.dot(order, rows, preferred_element_type=jnp.float32)
        moved = moved.astype(jnp.bfloat16).reshape(-1, PLANE, shots, points)
        for at, out in enumerate(outs):
            out[:, c] = moved[at]


def relayout(me, spectra, k, n, wanted, after):
    shots, _, _, points = spectra.shape
    block = jax.ShapeDtypeStruct((PLANE, 2, shots, points), spectra.dtype)
    return pl.pallas_call(
        functools.partial(relayout_kernel, n, shots, wanted),
        grid=(1,),
        out_shape=[block] * len(wanted),
        in_specs=[
            smem_spec(),
            pl.BlockSpec((shots, 2, n, points), lambda _: (0, 0, k, 0)),
        ]
        + [any_spec()] * len(after),
        out_specs=[pl.BlockSpec(block.shape, lambda _: (0, 0, 0, 0))] * len(wanted),
        compiler_params=params(),
        cost_estimate=PACE,
        name="relayout",
    )(me, spectra, *after)


def join_kernel(count_in, *refs):
    out = refs[-1]
    for at in range(count_in):
        out[at] = refs[at][...]


def join(blocks, after):
    block = blocks[0]
    return pl.pallas_call(
        functools.partial(join_kernel, len(blocks)),
        out_shape=jax.ShapeDtypeStruct((len(blocks), *block.shape), block.dtype),
        in_specs=[vmem_spec()] * len(blocks) + [any_spec()] * len(after),
        out_specs=vmem_spec(),
        compiler_params=params(),
        cost_estimate=COST,
        name="join",
    )(*blocks, *after)


def release_kernel(count, *refs):
    for block, out in zip(refs[:count], refs[-count:]):
        out[...] = block[...]


def release(blocks, after):
    return pl.pallas_call(
        functools.partial(release_kernel, len(blocks)),
        out_shape=[jax.ShapeDtypeStruct(block.shape, block.dtype) for block in blocks],
        in_specs=[vmem_spec()] * len(blocks) + [any_spec()] * len(after),
        out_specs=[vmem_spec()] * len(blocks),
        compiler_params=params(),
        cost_estimate=PACE,
        name="release",
    )(*blocks, *after)


def product_kernel(k, n, planes, me_ref, wave_ref, fold_row_ref, fold_col_ref, *refs):
    near_ref, far_ref, core_ref = refs[:3]
    outs, raw_ref, full_ref = refs[-planes - 2 : -2], refs[-2], refs[-1]
    me = me_ref[0]
    shots, points = near_ref.shape[3:]

    def rows_of(j, i):
        start = ((PLANE * j + i) ^ me) * shots
        return pl.ds(pl.multiple_of(start, shots), shots)

    def block(j, i, b, c):
        if i % 2:
            return core_ref[i // 2, j, b, c]
        return (far_ref if i // 2 else near_ref)[j, b, c]

    s = lax.broadcasted_iota(jnp.int32, (points, points), 0)
    x = lax.broadcasted_iota(jnp.int32, (points, points), 1)
    apart = jnp.abs(x - s)
    recorded = apart < fold_col_ref[...]
    mirrored = apart < fold_row_ref[...]

    def dot(left, right):
        return jnp.dot(left, right, preferred_element_type=jnp.float32)

    half = planes * shots
    for b in range(PLANE):
        for c in range(2):
            for j in range(planes):
                for i in range(PLANE):
                    raw_ref[b, c, rows_of(j, i), :] = block(j, i, b, c)
            own = raw_ref[b, c].astype(jnp.float32)
            full_ref[b, c] = jnp.where(
                recorded, own, jnp.where(mirrored, own.T, 0.0)
            ).astype(jnp.bfloat16)
        left = jnp.concatenate(
            [full_ref[b, c, rows_of(j, 0), :] for c in range(2) for j in range(planes)],
            axis=0,
        )
        by_re, by_im = dot(left, full_ref[b, 0]), dot(left, full_ref[b, 1])
        prod_re = by_re[:half] - by_im[half:]
        prod_im = by_im[:half] + by_re[half:]
        which = k * n + (me // PLANE) * PLANE + b
        wave_re, wave_im = wave_ref[0, which], wave_ref[1, which]
        made_re = (-(wave_re * prod_re - wave_im * prod_im)).astype(jnp.bfloat16)
        made_im = (-(wave_re * prod_im + wave_im * prod_re)).astype(jnp.bfloat16)
        for j, out in enumerate(outs):
            out[b, 0] = made_re[j * shots : (j + 1) * shots]
            out[b, 1] = made_im[j * shots : (j + 1) * shots]


def product(me, wave, fold, near, far, core, k, n, after):
    planes, _, _, shots, points = near.shape
    block = jax.ShapeDtypeStruct(near.shape[1:], near.dtype)
    return pl.pallas_call(
        functools.partial(product_kernel, k, n, planes),
        out_shape=[block] * planes,
        in_specs=[smem_spec()] * 2 + [vmem_spec()] * 5 + [any_spec()] * len(after),
        out_specs=[vmem_spec()] * planes,
        scratch_shapes=[pltpu.VMEM((PLANE, 2, points, points), jnp.bfloat16)] * 2,
        compiler_params=params(),
        cost_estimate=COST,
        name="product",
    )(me, wave, fold.reshape(1, -1), fold.reshape(-1, 1), near, far, core, *after)


def send(block, n, offset, what):
    with jax.named_scope(what):
        return lax.ppermute(block, "shot", [(d, d ^ offset) for d in range(n)])


def chunked_shards(n, spectra, fold_counts, inverse_wavelet):
    bins = spectra.shape[2]
    chunks, planes = bins // n, n // PLANE
    cross = list(reversed(range(planes // 2, planes)))
    rest = list(range(1, planes // 2))
    me = lax.axis_index("shot").astype(jnp.int32).reshape(1)

    last = []
    crossed = []

    def order():
        return last[-1:] + crossed[-2:-1]

    def depart(blocks, what):
        for j, block in blocks.items():
            if j:
                blocks[j] = send(block, n, PLANE * j, f"{what}_z{j}")
            if j in cross:
                crossed.append(blocks[j])
        return blocks

    arrived = [{} for _ in range(chunks)]
    beside = [{} for _ in range(chunks)]
    made = [{} for _ in range(chunks)]
    leaving = [{} for _ in range(chunks)]
    result, merge = [None], []

    def parts(at):
        return [cross[at]] + (([0] + rest) if at == len(cross) - 1 else [])

    def go_in(k, at):
        if k >= chunks:
            return
        wanted = parts(at)
        with jax.named_scope(f"in{k}_{at}"):
            blocks = relayout(me, spectra, k, n, wanted, order())
        last.append(blocks[0])
        arrived[k].update(depart(dict(zip(wanted, blocks)), f"in{k}"))

    def go_out(k, at):
        if not 0 <= k < chunks:
            return
        wanted = parts(at)
        with jax.named_scope(f"out{k}_{at}"):
            blocks = release([made[k][j] for j in wanted], order())
        last.append(blocks[0])
        leaving[k].update(depart(dict(zip(wanted, blocks)), f"out{k}"))

    def go_y(k):
        if not 0 <= k < chunks:
            return
        with jax.named_scope(f"y{k}"):
            near = join([arrived[k][j] for j in range(planes)], last[-1:])
        last.append(near)
        beside[k] = near, send(near, n, 2, f"in{k}_y")

    def go_core(k):
        if not 0 <= k < chunks:
            return
        with jax.named_scope(f"core{k}"):
            both = join(beside[k], last[-1:])
        last.append(both)
        beside[k] += (send(both, n, 1, f"in{k}_core"),)

    def multiply(k):
        if not 0 <= k < chunks:
            return
        with jax.named_scope(f"chunk{k}"):
            blocks = product(
                me, inverse_wavelet, fold_counts, *beside[k], k, n, last[-1:]
            )
        last.append(blocks[0])
        made[k] = dict(enumerate(blocks))

    begun = {}

    def begin_finish(k):
        if not 0 <= k < chunks:
            return
        blocks = {j: leaving[k][j] for j in range(planes) if j != cross[-1]}
        with jax.named_scope(f"chunk{k}"):
            begun[k] = early(
                merge[0], blocks, last[-1:], PACE if k == chunks - 2 else COST
            )
        last.append(begun[k])

    def finish(k):
        if not 0 <= k < chunks:
            return
        blocks = {cross[-1]: leaving[k][cross[-1]]}
        with jax.named_scope(f"chunk{k}"):
            result[0] = assemble(merge[0], begun[k], blocks, result[0], k, n, bins, [])

    for t in range(chunks):
        for at in range(len(cross)):
            go_in(t, at)
            if at == 0:
                multiply(t - 3)
        go_core(t - 2)
        if t == 1:
            merge.append(merge_order(me, n, spectra.shape[0], last[-1:]))
            last.append(merge[0])
        go_y(t - 1)
    for t in range(chunks):
        go_out(t, 0)
        if t == 0:
            multiply(chunks - 3)
        else:
            go_core(chunks - 3 + t)
            go_y(chunks - 2 + t)
        go_out(t, 1)
        if t:
            multiply(chunks - 3 + t)
        begin_finish(t - 1)
        finish(t - 1)
    begin_finish(chunks - 1)
    finish(chunks - 1)
    return result[0]


def solution(mesh):
    n = mesh.shape["shot"]

    def shards(spectra, fold_counts, inverse_wavelet):
        shots, _, bins, _ = spectra.shape
        power = n & (n - 1) == 0
        if power and n % 16 == 0 and bins % n == 0 and shots % 16 == 0:
            return chunked_shards(n, spectra, fold_counts, inverse_wavelet)
        return plain_shards(spectra, fold_counts, inverse_wavelet)

    in_specs = (P(("groups", "shot"), None, None, None), P("groups"), P())
    out_specs = P(("groups", "shot"), None, None, None)
    return jax.shard_map(
        shards, mesh=mesh, in_specs=in_specs, out_specs=out_specs, check_vma=False
    )
```

```python
import functools

import jax
import jax.numpy as jnp
from jax import lax
from jax.experimental import pallas as pl
from jax.experimental.pallas import tpu as pltpu
from jax.sharding import PartitionSpec as P

PLANE = 4
VMEM_LIMIT = 32 * 1024 * 1024


def batched_product(left_operand, right_operand):
    return jnp.einsum(
        "hwi,iwc->hwc", left_operand, right_operand, preferred_element_type=jnp.float32
    )


def plain_shards(spectra, fold_counts, inverse_wavelet):
    points = spectra.shape[3]
    everyone = jnp.arange(points, dtype=jnp.int32)
    regrouped = lax.all_to_all(spectra, "shot", split_axis=2, concat_axis=0, tiled=True)
    recorded = jnp.abs(everyone[None, :] - everyone[:, None]) < fold_counts[:, None]
    flipped = regrouped.transpose(3, 1, 2, 0)
    regrouped = jnp.where(
        recorded[:, None, None, :],
        regrouped,
        jnp.where(recorded.T[:, None, None, :], flipped, jnp.zeros_like(regrouped)),
    )
    local_bins = regrouped.shape[2]
    real_component = regrouped[:, 0]
    imaginary_component = regrouped[:, 1]
    prod_real = batched_product(real_component, real_component) - batched_product(
        imaginary_component, imaginary_component
    )
    prod_imag = batched_product(real_component, imaginary_component) + batched_product(
        imaginary_component, real_component
    )
    first_bin = lax.axis_index("shot") * local_bins
    wave = lax.dynamic_slice_in_dim(inverse_wavelet, first_bin, local_bins, 1)
    wavelet_real = wave[0][None, :, None]
    wave_imag = wave[1][None, :, None]
    output_real = -(wavelet_real * prod_real - wave_imag * prod_imag)
    out_imag = -(wavelet_real * prod_imag + wave_imag * prod_real)
    result = jnp.stack([output_real, out_imag], axis=1).astype(jnp.bfloat16)
    return lax.all_to_all(result, "shot", split_axis=0, concat_axis=2, tiled=True)


def any_spec():
    return pl.BlockSpec(memory_space=pl.ANY)


def vmem_spec():
    return pl.BlockSpec(memory_space=pltpu.VMEM)


def hbm_spec():
    return pl.BlockSpec(memory_space=pltpu.HBM)


def smem_spec():
    return pl.BlockSpec(memory_space=pltpu.SMEM)


def params():
    return pltpu.CompilerParams(vmem_limit_bytes=VMEM_LIMIT)


COST = pl.CostEstimate(flops=0, bytes_accessed=0, transcendentals=0)
PACE = pl.CostEstimate(flops=40_000_000_000, bytes_accessed=0, transcendentals=0)


def split_order(me, n, shots, wanted):
    rows, count = n * shots, PLANE * shots
    source = lax.broadcasted_iota(jnp.int32, (count, rows), 1)
    target = lax.broadcasted_iota(jnp.int32, (count, rows), 0)
    parts = []
    for j in wanted:
        which = ((me // PLANE) ^ j) * PLANE + target // shots
        parts.append((target % shots) * n + which == source)
    return jnp.concatenate(
        [jnp.where(part, 1.0, 0.0).astype(jnp.bfloat16) for part in parts], axis=0
    )


def merge_order_kernel(n, shots, me_ref, *refs):
    out = refs[-1]
    planes, rows, count = out.shape
    source = lax.broadcasted_iota(jnp.int32, (rows, count), 1)
    target = lax.broadcasted_iota(jnp.int32, (rows, count), 0)
    for j in range(planes):
        first = ((me_ref[0] // PLANE) ^ j) * PLANE
        hit = (target % n - first) * shots + target // n == source
        out[j] = jnp.where(hit, 1.0, 0.0).astype(jnp.bfloat16)


def merge_order(me, n, shots, after):
    return pl.pallas_call(
        functools.partial(merge_order_kernel, n, shots),
        out_shape=jax.ShapeDtypeStruct(
            (n // PLANE, n * shots, PLANE * shots), jnp.bfloat16
        ),
        in_specs=[smem_spec()] + [any_spec()] * len(after),
        out_specs=vmem_spec(),
        compiler_params=params(),
        cost_estimate=COST,
        name="merge_order",
    )(me, *after)


def merged(order_ref, blocks, c):
    total = None
    for j, block in blocks:
        rows = block[:, c].reshape(-1, block.shape[3])
        part = jnp.dot(order_ref[j], rows, preferred_element_type=jnp.float32)
        total = part if total is None else total + part
    return total


def early_kernel(which, order_ref, *refs):
    ins, out = refs[: len(which)], refs[-1]
    for c in range(2):
        out[c] = merged(order_ref, list(zip(which, ins)), c).astype(jnp.bfloat16)


def early(order, blocks, after, cost):
    _, _, shots, points = next(iter(blocks.values())).shape
    return pl.pallas_call(
        functools.partial(early_kernel, list(blocks)),
        out_shape=jax.ShapeDtypeStruct((2, order.shape[1], points), jnp.bfloat16),
        in_specs=[vmem_spec()] * (1 + len(blocks)) + [any_spec()] * len(after),
        out_specs=vmem_spec(),
        compiler_params=params(),
        cost_estimate=cost,
        name="early",
    )(order, *blocks.values(), *after)


def assemble_kernel(n, shots, k, which, order_ref, begun_ref, *refs):
    ins = refs[: len(which)]
    out, held, sems = refs[-3:]
    copies = []
    for c in range(2):
        total = merged(order_ref, list(zip(which, ins)), c)
        total = total + begun_ref[c].astype(jnp.float32)
        held[c] = total.astype(jnp.bfloat16).reshape(shots, n, -1)
        copies.append(
            pltpu.make_async_copy(
                held.at[c], out.at[:, c, pl.ds(k * n, n), :], sems.at[c]
            )
        )
        copies[c].start()
    for copy in copies:
        copy.wait()


def assemble(order, begun, blocks, result, k, n, bins, after):
    _, _, shots, points = next(iter(blocks.values())).shape
    extra = [] if result is None else [result]
    return pl.pallas_call(
        functools.partial(assemble_kernel, n, shots, k, list(blocks)),
        out_shape=jax.ShapeDtypeStruct((shots, 2, bins, points), jnp.bfloat16),
        in_specs=[vmem_spec()] * (2 + len(blocks))
        + [hbm_spec()] * len(extra)
        + [any_spec()] * len(after),
        out_specs=hbm_spec(),
        scratch_shapes=[
            pltpu.VMEM((2, shots, n, points), jnp.bfloat16),
            pltpu.SemaphoreType.DMA((2,)),
        ],
        input_output_aliases={2 + len(blocks): 0} if extra else {},
        compiler_params=params(),
        cost_estimate=COST,
        name="assemble",
    )(order, begun, *blocks.values(), *extra, *after)


def relayout_kernel(n, shots, wanted, me_ref, x_ref, *refs):
    outs = refs[-len(wanted) :]
    me = me_ref[0]
    order = split_order(me, n, shots, wanted)
    points = x_ref.shape[3]
    for c in range(2):
        rows = x_ref[:, c].reshape(shots * n, points)
        moved = jnp.dot(order, rows, preferred_element_type=jnp.float32)
        moved = moved.astype(jnp.bfloat16).reshape(-1, PLANE, shots, points)
        for at, out in enumerate(outs):
            out[:, c] = moved[at]


def relayout(me, spectra, k, n, wanted, after):
    shots, _, _, points = spectra.shape
    block = jax.ShapeDtypeStruct((PLANE, 2, shots, points), spectra.dtype)
    return pl.pallas_call(
        functools.partial(relayout_kernel, n, shots, wanted),
        grid=(1,),
        out_shape=[block] * len(wanted),
        in_specs=[
            smem_spec(),
            pl.BlockSpec((shots, 2, n, points), lambda _: (0, 0, k, 0)),
        ]
        + [any_spec()] * len(after),
        out_specs=[pl.BlockSpec(block.shape, lambda _: (0, 0, 0, 0))] * len(wanted),
        compiler_params=params(),
        cost_estimate=PACE,
        name="relayout",
    )(me, spectra, *after)


def join_kernel(count_in, *refs):
    out = refs[-1]
    for at in range(count_in):
        out[at] = refs[at][...]


def join(blocks, after):
    block = blocks[0]
    return pl.pallas_call(
        functools.partial(join_kernel, len(blocks)),
        out_shape=jax.ShapeDtypeStruct((len(blocks), *block.shape), block.dtype),
        in_specs=[vmem_spec()] * len(blocks) + [any_spec()] * len(after),
        out_specs=vmem_spec(),
        compiler_params=params(),
        cost_estimate=COST,
        name="join",
    )(*blocks, *after)


def release_kernel(count, *refs):
    for block, out in zip(refs[:count], refs[-count:]):
        out[...] = block[...]


def release(blocks, after):
    return pl.pallas_call(
        functools.partial(release_kernel, len(blocks)),
        out_shape=[jax.ShapeDtypeStruct(block.shape, block.dtype) for block in blocks],
        in_specs=[vmem_spec()] * len(blocks) + [any_spec()] * len(after),
        out_specs=[vmem_spec()] * len(blocks),
        compiler_params=params(),
        cost_estimate=PACE,
        name="release",
    )(*blocks, *after)


def product_kernel(k, n, planes, me_ref, wave_ref, fold_row_ref, fold_col_ref, *refs):
    near_ref, far_ref, core_ref = refs[:3]
    outs, raw_ref, full_ref = refs[-planes - 2 : -2], refs[-2], refs[-1]
    me = me_ref[0]
    shots, points = near_ref.shape[3:]

    def rows_of(j, i):
        start = ((PLANE * j + i) ^ me) * shots
        return pl.ds(pl.multiple_of(start, shots), shots)

    def block(j, i, b, c):
        if i % 2:
            return core_ref[i // 2, j, b, c]
        return (far_ref if i // 2 else near_ref)[j, b, c]

    s = lax.broadcasted_iota(jnp.int32, (points, points), 0)
    x = lax.broadcasted_iota(jnp.int32, (points, points), 1)
    apart = jnp.abs(x - s)
    recorded = apart < fold_col_ref[...]
    mirrored = apart < fold_row_ref[...]

    def dot(left, right):
        return jnp.dot(left, right, preferred_element_type=jnp.float32)

    half = planes * shots
    for b in range(PLANE):
        for c in range(2):
            for j in range(planes):
                for i in range(PLANE):
                    raw_ref[b, c, rows_of(j, i), :] = block(j, i, b, c)
            own = raw_ref[b, c].astype(jnp.float32)
            full_ref[b, c] = jnp.where(
                recorded, own, jnp.where(mirrored, own.T, 0.0)
            ).astype(jnp.bfloat16)
        left = jnp.concatenate(
            [full_ref[b, c, rows_of(j, 0), :] for c in range(2) for j in range(planes)],
            axis=0,
        )
        by_re, by_im = dot(left, full_ref[b, 0]), dot(left, full_ref[b, 1])
        prod_re = by_re[:half] - by_im[half:]
        prod_im = by_im[:half] + by_re[half:]
        which = k * n + (me // PLANE) * PLANE + b
        wave_re, wave_im = wave_ref[0, which], wave_ref[1, which]
        made_re = (-(wave_re * prod_re - wave_im * prod_im)).astype(jnp.bfloat16)
        made_im = (-(wave_re * prod_im + wave_im * prod_re)).astype(jnp.bfloat16)
        for j, out in enumerate(outs):
            out[b, 0] = made_re[j * shots : (j + 1) * shots]
            out[b, 1] = made_im[j * shots : (j + 1) * shots]


def product(me, wave, fold, near, far, core, k, n, after):
    planes, _, _, shots, points = near.shape
    block = jax.ShapeDtypeStruct(near.shape[1:], near.dtype)
    return pl.pallas_call(
        functools.partial(product_kernel, k, n, planes),
        out_shape=[block] * planes,
        in_specs=[smem_spec()] * 2 + [vmem_spec()] * 5 + [any_spec()] * len(after),
        out_specs=[vmem_spec()] * planes,
        scratch_shapes=[pltpu.VMEM((PLANE, 2, points, points), jnp.bfloat16)] * 2,
        compiler_params=params(),
        cost_estimate=COST,
        name="product",
    )(me, wave, fold.reshape(1, -1), fold.reshape(-1, 1), near, far, core, *after)


def send(block, n, offset, what):
    with jax.named_scope(what):
        return lax.ppermute(block, "shot", [(d, d ^ offset) for d in range(n)])


def chunked_shards(n, spectra, fold_counts, inverse_wavelet):
    bins = spectra.shape[2]
    chunks, planes = bins // n, n // PLANE
    cross = list(reversed(range(planes // 2, planes)))
    rest = list(range(1, planes // 2))
    me = lax.axis_index("shot").astype(jnp.int32).reshape(1)

    last = []
    crossed = []

    def order():
        return last[-1:] + crossed[-2:-1]

    def depart(blocks, what):
        for j, block in blocks.items():
            if j:
                blocks[j] = send(block, n, PLANE * j, f"{what}_z{j}")
            if j in cross:
                crossed.append(blocks[j])
        return blocks

    arrived = [{} for _ in range(chunks)]
    beside = [{} for _ in range(chunks)]
    made = [{} for _ in range(chunks)]
    leaving = [{} for _ in range(chunks)]
    result, merge = [None], []

    def parts(at):
        return [cross[at]] + (([0] + rest) if at == len(cross) - 1 else [])

    def go_in(k, at):
        if k >= chunks:
            return
        wanted = parts(at)
        with jax.named_scope(f"in{k}_{at}"):
            blocks = relayout(me, spectra, k, n, wanted, order())
        last.append(blocks[0])
        arrived[k].update(depart(dict(zip(wanted, blocks)), f"in{k}"))

    def go_out(k, at):
        if not 0 <= k < chunks:
            return
        wanted = parts(at)
        with jax.named_scope(f"out{k}_{at}"):
            blocks = release([made[k][j] for j in wanted], order())
        last.append(blocks[0])
        leaving[k].update(depart(dict(zip(wanted, blocks)), f"out{k}"))

    def go_y(k):
        if not 0 <= k < chunks:
            return
        with jax.named_scope(f"y{k}"):
            near = join([arrived[k][j] for j in range(planes)], last[-1:])
        last.append(near)
        beside[k] = near, send(near, n, 2, f"in{k}_y")

    def go_core(k):
        if not 0 <= k < chunks:
            return
        with jax.named_scope(f"core{k}"):
            both = join(beside[k], last[-1:])
        last.append(both)
        beside[k] += (send(both, n, 1, f"in{k}_core"),)

    def multiply(k):
        if not 0 <= k < chunks:
            return
        with jax.named_scope(f"chunk{k}"):
            blocks = product(
                me, inverse_wavelet, fold_counts, *beside[k], k, n, last[-1:]
            )
        last.append(blocks[0])
        made[k] = dict(enumerate(blocks))

    begun = {}

    def begin_finish(k):
        if not 0 <= k < chunks:
            return
        blocks = {j: leaving[k][j] for j in range(planes) if j != cross[-1]}
        with jax.named_scope(f"chunk{k}"):
            begun[k] = early(
                merge[0], blocks, last[-1:], PACE if k == chunks - 2 else COST
            )
        last.append(begun[k])

    def finish(k):
        if not 0 <= k < chunks:
            return
        blocks = {cross[-1]: leaving[k][cross[-1]]}
        with jax.named_scope(f"chunk{k}"):
            result[0] = assemble(merge[0], begun[k], blocks, result[0], k, n, bins, [])

    for t in range(chunks):
        for at in range(len(cross)):
            go_in(t, at)
            if at == 0:
                multiply(t - 3)
        go_core(t - 2)
        if t == 1:
            merge.append(merge_order(me, n, spectra.shape[0], last[-1:]))
            last.append(merge[0])
        go_y(t - 1)
    for t in range(chunks):
        go_out(t, 0)
        if t == 0:
            multiply(chunks - 3)
        else:
            go_core(chunks - 3 + t)
            go_y(chunks - 2 + t)
        go_out(t, 1)
        if t:
            multiply(chunks - 3 + t)
        begin_finish(t - 1)
        finish(t - 1)
    begin_finish(chunks - 1)
    finish(chunks - 1)
    return result[0]


def solution(mesh):
    n = mesh.shape["shot"]

    def shards(spectra, fold_counts, inverse_wavelet):
        shots, _, bins, _ = spectra.shape
        if n == 4 * PLANE and bins % n == 0 and bins // n >= 4 and shots % 16 == 0:
            return chunked_shards(n, spectra, fold_counts, inverse_wavelet)
        return plain_shards(spectra, fold_counts, inverse_wavelet)

    in_specs = (P(("groups", "shot"), None, None, None), P("groups"), P())
    out_specs = P(("groups", "shot"), None, None, None)
    return jax.shard_map(
        shards, mesh=mesh, in_specs=in_specs, out_specs=out_specs, check_vma=False
    )
```

```python
import functools

import jax
import jax.numpy as jnp
from jax import lax
from jax.experimental import pallas as pl
from jax.experimental.pallas import tpu as pltpu
from jax.sharding import PartitionSpec as P

PLANE = 4
VMEM_LIMIT = 32 * 1024 * 1024


def batched_product(left_operand, right_operand):
    return jnp.einsum(
        "hwi,iwc->hwc", left_operand, right_operand, preferred_element_type=jnp.float32
    )


def plain_shards(spectra, fold_counts, inverse_wavelet):
    points = spectra.shape[3]
    everyone = jnp.arange(points, dtype=jnp.int32)
    regrouped = lax.all_to_all(spectra, "shot", split_axis=2, concat_axis=0, tiled=True)
    recorded = jnp.abs(everyone[None, :] - everyone[:, None]) < fold_counts[:, None]
    flipped = regrouped.transpose(3, 1, 2, 0)
    regrouped = jnp.where(
        recorded[:, None, None, :],
        regrouped,
        jnp.where(recorded.T[:, None, None, :], flipped, jnp.zeros_like(regrouped)),
    )
    local_bins = regrouped.shape[2]
    real_component = regrouped[:, 0]
    imaginary_component = regrouped[:, 1]
    prod_real = batched_product(real_component, real_component) - batched_product(
        imaginary_component, imaginary_component
    )
    prod_imag = batched_product(real_component, imaginary_component) + batched_product(
        imaginary_component, real_component
    )
    first_bin = lax.axis_index("shot") * local_bins
    wave = lax.dynamic_slice_in_dim(inverse_wavelet, first_bin, local_bins, 1)
    wavelet_real = wave[0][None, :, None]
    wave_imag = wave[1][None, :, None]
    output_real = -(wavelet_real * prod_real - wave_imag * prod_imag)
    out_imag = -(wavelet_real * prod_imag + wave_imag * prod_real)
    result = jnp.stack([output_real, out_imag], axis=1).astype(jnp.bfloat16)
    return lax.all_to_all(result, "shot", split_axis=0, concat_axis=2, tiled=True)


def any_spec():
    return pl.BlockSpec(memory_space=pl.ANY)


def vmem_spec():
    return pl.BlockSpec(memory_space=pltpu.VMEM)


def hbm_spec():
    return pl.BlockSpec(memory_space=pltpu.HBM)


def smem_spec():
    return pl.BlockSpec(memory_space=pltpu.SMEM)


def params():
    return pltpu.CompilerParams(vmem_limit_bytes=VMEM_LIMIT)


COST = pl.CostEstimate(flops=0, bytes_accessed=0, transcendentals=0)
PACE = pl.CostEstimate(flops=40_000_000_000, bytes_accessed=0, transcendentals=0)


def split_order(me, n, shots, wanted):
    rows, count = n * shots, PLANE * shots
    source = lax.broadcasted_iota(jnp.int32, (count, rows), 1)
    target = lax.broadcasted_iota(jnp.int32, (count, rows), 0)
    parts = []
    for j in wanted:
        which = ((me // PLANE) ^ j) * PLANE + target // shots
        parts.append((target % shots) * n + which == source)
    return jnp.concatenate(
        [jnp.where(part, 1.0, 0.0).astype(jnp.bfloat16) for part in parts], axis=0
    )


def merge_order_kernel(n, shots, me_ref, *refs):
    out = refs[-1]
    planes, rows, count = out.shape
    source = lax.broadcasted_iota(jnp.int32, (rows, count), 1)
    target = lax.broadcasted_iota(jnp.int32, (rows, count), 0)
    for j in range(planes):
        first = ((me_ref[0] // PLANE) ^ j) * PLANE
        hit = (target % n - first) * shots + target // n == source
        out[j] = jnp.where(hit, 1.0, 0.0).astype(jnp.bfloat16)


def merge_order(me, n, shots, after):
    return pl.pallas_call(
        functools.partial(merge_order_kernel, n, shots),
        out_shape=jax.ShapeDtypeStruct(
            (n // PLANE, n * shots, PLANE * shots), jnp.bfloat16
        ),
        in_specs=[smem_spec()] + [any_spec()] * len(after),
        out_specs=vmem_spec(),
        compiler_params=params(),
        cost_estimate=COST,
        name="merge_order",
    )(me, *after)


def merged(order_ref, blocks, c):
    total = None
    for j, block in blocks:
        rows = block[:, c].reshape(-1, block.shape[3])
        part = jnp.dot(order_ref[j], rows, preferred_element_type=jnp.float32)
        total = part if total is None else total + part
    return total


def early_kernel(which, order_ref, *refs):
    ins, out = refs[: len(which)], refs[-1]
    for c in range(2):
        out[c] = merged(order_ref, list(zip(which, ins)), c).astype(jnp.bfloat16)


def early(order, blocks, after, cost):
    _, _, shots, points = next(iter(blocks.values())).shape
    return pl.pallas_call(
        functools.partial(early_kernel, list(blocks)),
        out_shape=jax.ShapeDtypeStruct((2, order.shape[1], points), jnp.bfloat16),
        in_specs=[vmem_spec()] * (1 + len(blocks)) + [any_spec()] * len(after),
        out_specs=vmem_spec(),
        compiler_params=params(),
        cost_estimate=cost,
        name="early",
    )(order, *blocks.values(), *after)


def assemble_kernel(n, shots, k, which, order_ref, begun_ref, *refs):
    ins = refs[: len(which)]
    out, held, sems = refs[-3:]
    copies = []
    for c in range(2):
        total = merged(order_ref, list(zip(which, ins)), c)
        total = total + begun_ref[c].astype(jnp.float32)
        held[c] = total.astype(jnp.bfloat16).reshape(shots, n, -1)
        copies.append(
            pltpu.make_async_copy(
                held.at[c], out.at[:, c, pl.ds(k * n, n), :], sems.at[c]
            )
        )
        copies[c].start()
    for copy in copies:
        copy.wait()


def assemble(order, begun, blocks, result, k, n, bins, after):
    _, _, shots, points = next(iter(blocks.values())).shape
    extra = [] if result is None else [result]
    return pl.pallas_call(
        functools.partial(assemble_kernel, n, shots, k, list(blocks)),
        out_shape=jax.ShapeDtypeStruct((shots, 2, bins, points), jnp.bfloat16),
        in_specs=[vmem_spec()] * (2 + len(blocks))
        + [hbm_spec()] * len(extra)
        + [any_spec()] * len(after),
        out_specs=hbm_spec(),
        scratch_shapes=[
            pltpu.VMEM((2, shots, n, points), jnp.bfloat16),
            pltpu.SemaphoreType.DMA((2,)),
        ],
        input_output_aliases={2 + len(blocks): 0} if extra else {},
        compiler_params=params(),
        cost_estimate=COST,
        name="assemble",
    )(order, begun, *blocks.values(), *extra, *after)


def relayout_kernel(n, shots, wanted, me_ref, x_ref, *refs):
    outs = refs[-len(wanted) :]
    me = me_ref[0]
    order = split_order(me, n, shots, wanted)
    points = x_ref.shape[3]
    for c in range(2):
        rows = x_ref[:, c].reshape(shots * n, points)
        moved = jnp.dot(order, rows, preferred_element_type=jnp.float32)
        moved = moved.astype(jnp.bfloat16).reshape(-1, PLANE, shots, points)
        for at, out in enumerate(outs):
            out[:, c] = moved[at]


def relayout(me, spectra, k, n, wanted, after):
    shots, _, _, points = spectra.shape
    block = jax.ShapeDtypeStruct((PLANE, 2, shots, points), spectra.dtype)
    return pl.pallas_call(
        functools.partial(relayout_kernel, n, shots, wanted),
        grid=(1,),
        out_shape=[block] * len(wanted),
        in_specs=[
            smem_spec(),
            pl.BlockSpec((shots, 2, n, points), lambda _: (0, 0, k, 0)),
        ]
        + [any_spec()] * len(after),
        out_specs=[pl.BlockSpec(block.shape, lambda _: (0, 0, 0, 0))] * len(wanted),
        compiler_params=params(),
        cost_estimate=PACE,
        name="relayout",
    )(me, spectra, *after)


def join_kernel(count_in, *refs):
    out = refs[-1]
    for at in range(count_in):
        out[at] = refs[at][...]


def join(blocks, after):
    block = blocks[0]
    return pl.pallas_call(
        functools.partial(join_kernel, len(blocks)),
        out_shape=jax.ShapeDtypeStruct((len(blocks), *block.shape), block.dtype),
        in_specs=[vmem_spec()] * len(blocks) + [any_spec()] * len(after),
        out_specs=vmem_spec(),
        compiler_params=params(),
        cost_estimate=COST,
        name="join",
    )(*blocks, *after)


def release_kernel(count, *refs):
    for block, out in zip(refs[:count], refs[-count:]):
        out[...] = block[...]


def release(blocks, after):
    return pl.pallas_call(
        functools.partial(release_kernel, len(blocks)),
        out_shape=[jax.ShapeDtypeStruct(block.shape, block.dtype) for block in blocks],
        in_specs=[vmem_spec()] * len(blocks) + [any_spec()] * len(after),
        out_specs=[vmem_spec()] * len(blocks),
        compiler_params=params(),
        cost_estimate=PACE,
        name="release",
    )(*blocks, *after)


def product_kernel(k, n, planes, me_ref, wave_ref, fold_row_ref, fold_col_ref, *refs):
    near_ref, far_ref, core_ref = refs[:3]
    outs, raw_ref, full_ref = refs[-planes - 2 : -2], refs[-2], refs[-1]
    me = me_ref[0]
    shots, points = near_ref.shape[3:]

    def rows_of(j, i):
        start = ((PLANE * j + i) ^ me) * shots
        return pl.ds(pl.multiple_of(start, shots), shots)

    def block(j, i, b, c):
        if i % 2:
            return core_ref[i // 2, j, b, c]
        return (far_ref if i // 2 else near_ref)[j, b, c]

    s = lax.broadcasted_iota(jnp.int32, (points, points), 0)
    x = lax.broadcasted_iota(jnp.int32, (points, points), 1)
    apart = jnp.abs(x - s)
    recorded = apart < fold_col_ref[...]
    mirrored = apart < fold_row_ref[...]

    def dot(left, right):
        return jnp.dot(left, right, preferred_element_type=jnp.float32)

    half = planes * shots
    for b in range(PLANE):
        for c in range(2):
            for j in range(planes):
                for i in range(PLANE):
                    raw_ref[b, c, rows_of(j, i), :] = block(j, i, b, c)
            own = raw_ref[b, c].astype(jnp.float32)
            full_ref[b, c] = jnp.where(
                recorded, own, jnp.where(mirrored, own.T, 0.0)
            ).astype(jnp.bfloat16)
        left = jnp.concatenate(
            [full_ref[b, c, rows_of(j, 0), :] for c in range(2) for j in range(planes)],
            axis=0,
        )
        by_re, by_im = dot(left, full_ref[b, 0]), dot(left, full_ref[b, 1])
        prod_re = by_re[:half] - by_im[half:]
        prod_im = by_im[:half] + by_re[half:]
        which = k * n + (me // PLANE) * PLANE + b
        wave_re, wave_im = wave_ref[0, which], wave_ref[1, which]
        made_re = (-(wave_re * prod_re - wave_im * prod_im)).astype(jnp.bfloat16)
        made_im = (-(wave_re * prod_im + wave_im * prod_re)).astype(jnp.bfloat16)
        for j, out in enumerate(outs):
            out[b, 0] = made_re[j * shots : (j + 1) * shots]
            out[b, 1] = made_im[j * shots : (j + 1) * shots]


def product(me, wave, fold, near, far, core, k, n, after):
    planes, _, _, shots, points = near.shape
    block = jax.ShapeDtypeStruct(near.shape[1:], near.dtype)
    return pl.pallas_call(
        functools.partial(product_kernel, k, n, planes),
        out_shape=[block] * planes,
        in_specs=[smem_spec()] * 2 + [vmem_spec()] * 5 + [any_spec()] * len(after),
        out_specs=[vmem_spec()] * planes,
        scratch_shapes=[pltpu.VMEM((PLANE, 2, points, points), jnp.bfloat16)] * 2,
        compiler_params=params(),
        cost_estimate=COST,
        name="product",
    )(me, wave, fold.reshape(1, -1), fold.reshape(-1, 1), near, far, core, *after)


def send(block, n, offset, what):
    with jax.named_scope(what):
        return lax.ppermute(block, "shot", [(d, d ^ offset) for d in range(n)])


def chunked_shards(n, spectra, fold_counts, inverse_wavelet):
    bins = spectra.shape[2]
    chunks, planes = bins // n, n // PLANE
    cross = list(reversed(range(planes // 2, planes)))
    rest = list(range(1, planes // 2))
    me = lax.axis_index("shot").astype(jnp.int32).reshape(1)

    last = []
    crossed = []

    def order():
        return last[-1:] + crossed[-2:-1]

    def depart(blocks, what):
        for j, block in blocks.items():
            if j:
                blocks[j] = send(block, n, PLANE * j, f"{what}_z{j}")
            if j in cross:
                crossed.append(blocks[j])
        return blocks

    arrived = [{} for _ in range(chunks)]
    beside = [{} for _ in range(chunks)]
    made = [{} for _ in range(chunks)]
    leaving = [{} for _ in range(chunks)]
    result, merge = [None], []
    first_chunk = lax.slice_in_dim(spectra, 0, n, axis=2)

    def parts(at):
        return [cross[at]] + (([0] + rest) if at == len(cross) - 1 else [])

    def go_in(k, at):
        if k >= chunks:
            return
        wanted = parts(at)
        with jax.named_scope(f"in{k}_{at}"):
            own, at_chunk = (spectra, k) if k else (first_chunk, 0)
            blocks = relayout(me, own, at_chunk, n, wanted, order())
        last.append(blocks[0])
        arrived[k].update(depart(dict(zip(wanted, blocks)), f"in{k}"))

    def go_out(k, at):
        if not 0 <= k < chunks:
            return
        wanted = parts(at)
        with jax.named_scope(f"out{k}_{at}"):
            blocks = release([made[k][j] for j in wanted], order())
        last.append(blocks[0])
        leaving[k].update(depart(dict(zip(wanted, blocks)), f"out{k}"))

    def go_y(k):
        if not 0 <= k < chunks:
            return
        with jax.named_scope(f"y{k}"):
            near = join([arrived[k][j] for j in range(planes)], last[-1:])
        last.append(near)
        beside[k] = near, send(near, n, 2, f"in{k}_y")

    def go_core(k):
        if not 0 <= k < chunks:
            return
        with jax.named_scope(f"core{k}"):
            both = join(beside[k], last[-1:])
        last.append(both)
        beside[k] += (send(both, n, 1, f"in{k}_core"),)

    def multiply(k):
        if not 0 <= k < chunks:
            return
        with jax.named_scope(f"chunk{k}"):
            blocks = product(
                me, inverse_wavelet, fold_counts, *beside[k], k, n, last[-1:]
            )
        last.append(blocks[0])
        made[k] = dict(enumerate(blocks))

    begun = {}

    def begin_finish(k):
        if not 0 <= k < chunks:
            return
        blocks = {j: leaving[k][j] for j in range(planes) if j != cross[-1]}
        with jax.named_scope(f"chunk{k}"):
            begun[k] = early(
                merge[0], blocks, last[-1:], PACE if k == chunks - 2 else COST
            )
        last.append(begun[k])

    def finish(k):
        if not 0 <= k < chunks:
            return
        blocks = {cross[-1]: leaving[k][cross[-1]]}
        with jax.named_scope(f"chunk{k}"):
            result[0] = assemble(merge[0], begun[k], blocks, result[0], k, n, bins, [])

    for t in range(chunks):
        for at in range(len(cross)):
            go_in(t, at)
            if at == 0:
                multiply(t - 3)
        go_core(t - 2)
        if t == 1:
            merge.append(merge_order(me, n, spectra.shape[0], last[-1:]))
            last.append(merge[0])
        go_y(t - 1)
    for t in range(chunks):
        go_out(t, 0)
        if t == 0:
            multiply(chunks - 3)
        else:
            go_core(chunks - 3 + t)
            go_y(chunks - 2 + t)
        go_out(t, 1)
        if t:
            multiply(chunks - 3 + t)
        begin_finish(t - 1)
        finish(t - 1)
    begin_finish(chunks - 1)
    finish(chunks - 1)
    return result[0]


def solution(mesh):
    n = mesh.shape["shot"]

    def shards(spectra, fold_counts, inverse_wavelet):
        shots, _, bins, _ = spectra.shape
        if n == 4 * PLANE and bins % n == 0 and bins // n >= 4 and shots % 16 == 0:
            return chunked_shards(n, spectra, fold_counts, inverse_wavelet)
        return plain_shards(spectra, fold_counts, inverse_wavelet)

    in_specs = (P(("groups", "shot"), None, None, None), P("groups"), P())
    out_specs = P(("groups", "shot"), None, None, None)
    return jax.shard_map(
        shards, mesh=mesh, in_specs=in_specs, out_specs=out_specs, check_vma=False
    )
```

```python
import functools

import jax
import jax.numpy as jnp
from jax import lax
from jax.experimental import pallas as pl
from jax.experimental.pallas import tpu as pltpu
from jax.sharding import PartitionSpec as P

PLANE = 4
VMEM_LIMIT = 32 * 1024 * 1024


def batched_product(left_operand, right_operand):
    return jnp.einsum(
        "hwi,iwc->hwc", left_operand, right_operand, preferred_element_type=jnp.float32
    )


def plain_shards(spectra, fold_counts, inverse_wavelet):
    points = spectra.shape[3]
    everyone = jnp.arange(points, dtype=jnp.int32)
    regrouped = lax.all_to_all(spectra, "shot", split_axis=2, concat_axis=0, tiled=True)
    recorded = jnp.abs(everyone[None, :] - everyone[:, None]) < fold_counts[:, None]
    flipped = regrouped.transpose(3, 1, 2, 0)
    regrouped = jnp.where(
        recorded[:, None, None, :],
        regrouped,
        jnp.where(recorded.T[:, None, None, :], flipped, jnp.zeros_like(regrouped)),
    )
    local_bins = regrouped.shape[2]
    real_component = regrouped[:, 0]
    imaginary_component = regrouped[:, 1]
    prod_real = batched_product(real_component, real_component) - batched_product(
        imaginary_component, imaginary_component
    )
    prod_imag = batched_product(real_component, imaginary_component) + batched_product(
        imaginary_component, real_component
    )
    first_bin = lax.axis_index("shot") * local_bins
    wave = lax.dynamic_slice_in_dim(inverse_wavelet, first_bin, local_bins, 1)
    wavelet_real = wave[0][None, :, None]
    wave_imag = wave[1][None, :, None]
    output_real = -(wavelet_real * prod_real - wave_imag * prod_imag)
    out_imag = -(wavelet_real * prod_imag + wave_imag * prod_real)
    result = jnp.stack([output_real, out_imag], axis=1).astype(jnp.bfloat16)
    return lax.all_to_all(result, "shot", split_axis=0, concat_axis=2, tiled=True)


def any_spec():
    return pl.BlockSpec(memory_space=pl.ANY)


def vmem_spec():
    return pl.BlockSpec(memory_space=pltpu.VMEM)


def hbm_spec():
    return pl.BlockSpec(memory_space=pltpu.HBM)


def smem_spec():
    return pl.BlockSpec(memory_space=pltpu.SMEM)


def params():
    return pltpu.CompilerParams(vmem_limit_bytes=VMEM_LIMIT)


COST = pl.CostEstimate(flops=0, bytes_accessed=0, transcendentals=0)
PACE = pl.CostEstimate(flops=40_000_000_000, bytes_accessed=0, transcendentals=0)


def split_order(me, n, shots, wanted):
    rows, count = n * shots, PLANE * shots
    source = lax.broadcasted_iota(jnp.int32, (count, rows), 1)
    target = lax.broadcasted_iota(jnp.int32, (count, rows), 0)
    parts = []
    for j in wanted:
        which = ((me // PLANE) ^ j) * PLANE + target // shots
        parts.append((target % shots) * n + which == source)
    return jnp.concatenate(
        [jnp.where(part, 1.0, 0.0).astype(jnp.bfloat16) for part in parts], axis=0
    )


def merge_order_kernel(n, shots, me_ref, *refs):
    out = refs[-1]
    planes, rows, count = out.shape
    source = lax.broadcasted_iota(jnp.int32, (rows, count), 1)
    target = lax.broadcasted_iota(jnp.int32, (rows, count), 0)
    for j in range(planes):
        first = ((me_ref[0] // PLANE) ^ j) * PLANE
        hit = (target % n - first) * shots + target // n == source
        out[j] = jnp.where(hit, 1.0, 0.0).astype(jnp.bfloat16)


def merge_order(me, n, shots, after):
    return pl.pallas_call(
        functools.partial(merge_order_kernel, n, shots),
        out_shape=jax.ShapeDtypeStruct(
            (n // PLANE, n * shots, PLANE * shots), jnp.bfloat16
        ),
        in_specs=[smem_spec()] + [any_spec()] * len(after),
        out_specs=vmem_spec(),
        compiler_params=params(),
        cost_estimate=COST,
        name="merge_order",
    )(me, *after)


def merged(order_ref, blocks, c):
    total = None
    for j, block in blocks:
        rows = block[:, c].reshape(-1, block.shape[3])
        part = jnp.dot(order_ref[j], rows, preferred_element_type=jnp.float32)
        total = part if total is None else total + part
    return total


def early_kernel(which, order_ref, *refs):
    ins, out = refs[: len(which)], refs[-1]
    for c in range(2):
        out[c] = merged(order_ref, list(zip(which, ins)), c).astype(jnp.bfloat16)


def early(order, blocks, after, cost):
    _, _, shots, points = next(iter(blocks.values())).shape
    return pl.pallas_call(
        functools.partial(early_kernel, list(blocks)),
        out_shape=jax.ShapeDtypeStruct((2, order.shape[1], points), jnp.bfloat16),
        in_specs=[vmem_spec()] * (1 + len(blocks)) + [any_spec()] * len(after),
        out_specs=vmem_spec(),
        compiler_params=params(),
        cost_estimate=cost,
        name="early",
    )(order, *blocks.values(), *after)


def assemble_kernel(n, shots, k, which, order_ref, begun_ref, *refs):
    ins = refs[: len(which)]
    out, held, sems = refs[-3:]
    copies = []
    for c in range(2):
        total = merged(order_ref, list(zip(which, ins)), c)
        total = total + begun_ref[c].astype(jnp.float32)
        held[c] = total.astype(jnp.bfloat16).reshape(shots, n, -1)
        copies.append(
            pltpu.make_async_copy(
                held.at[c], out.at[:, c, pl.ds(k * n, n), :], sems.at[c]
            )
        )
        copies[c].start()
    for copy in copies:
        copy.wait()


def assemble(order, begun, blocks, result, k, n, bins, after):
    _, _, shots, points = next(iter(blocks.values())).shape
    extra = [] if result is None else [result]
    return pl.pallas_call(
        functools.partial(assemble_kernel, n, shots, k, list(blocks)),
        out_shape=jax.ShapeDtypeStruct((shots, 2, bins, points), jnp.bfloat16),
        in_specs=[vmem_spec()] * (2 + len(blocks))
        + [hbm_spec()] * len(extra)
        + [any_spec()] * len(after),
        out_specs=hbm_spec(),
        scratch_shapes=[
            pltpu.VMEM((2, shots, n, points), jnp.bfloat16),
            pltpu.SemaphoreType.DMA((2,)),
        ],
        input_output_aliases={2 + len(blocks): 0} if extra else {},
        compiler_params=params(),
        cost_estimate=COST,
        name="assemble",
    )(order, begun, *blocks.values(), *extra, *after)


def relayout_kernel(n, shots, wanted, me_ref, x_ref, *refs):
    outs = refs[-len(wanted) :]
    me = me_ref[0]
    order = split_order(me, n, shots, wanted)
    points = x_ref.shape[3]
    for c in range(2):
        rows = x_ref[:, c].reshape(shots * n, points)
        moved = jnp.dot(order, rows, preferred_element_type=jnp.float32)
        moved = moved.astype(jnp.bfloat16).reshape(-1, PLANE, shots, points)
        for at, out in enumerate(outs):
            out[:, c] = moved[at]


def relayout(me, spectra, k, n, wanted, after):
    shots, _, _, points = spectra.shape
    block = jax.ShapeDtypeStruct((PLANE, 2, shots, points), spectra.dtype)
    return pl.pallas_call(
        functools.partial(relayout_kernel, n, shots, wanted),
        grid=(1,),
        out_shape=[block] * len(wanted),
        in_specs=[
            smem_spec(),
            pl.BlockSpec((shots, 2, n, points), lambda _: (0, 0, k, 0)),
        ]
        + [any_spec()] * len(after),
        out_specs=[pl.BlockSpec(block.shape, lambda _: (0, 0, 0, 0))] * len(wanted),
        compiler_params=params(),
        cost_estimate=PACE,
        name="relayout",
    )(me, spectra, *after)


def first_kernel(shots, wanted, me_ref, x_ref, out):
    width, points = x_ref.shape[2:]
    rows, count = shots * width, PLANE * shots
    source = lax.broadcasted_iota(jnp.int32, (count, rows), 1)
    target = lax.broadcasted_iota(jnp.int32, (count, rows), 0)
    plane = (me_ref[0] // PLANE) ^ wanted
    bins = (plane * PLANE) % width + target // shots
    hit = (target % shots) * width + bins == source
    order = jnp.where(hit, 1.0, 0.0).astype(jnp.bfloat16)
    for c in range(2):
        block = x_ref[:, c].reshape(rows, points)
        moved = jnp.dot(order, block, preferred_element_type=jnp.float32)
        out[:, c] = moved.astype(jnp.bfloat16).reshape(PLANE, shots, points)


def first(me, spectra, wanted):
    shots, _, _, points = spectra.shape
    width = 2 * PLANE
    start = (((me[0] // PLANE) ^ wanted) * PLANE) // width * width
    few = lax.dynamic_slice_in_dim(spectra, start, width, axis=2)
    return pl.pallas_call(
        functools.partial(first_kernel, shots, wanted),
        out_shape=jax.ShapeDtypeStruct((PLANE, 2, shots, points), spectra.dtype),
        in_specs=[smem_spec(), vmem_spec()],
        out_specs=vmem_spec(),
        compiler_params=params(),
        cost_estimate=PACE,
        name="first",
    )(me, few)


def join_kernel(count_in, *refs):
    out = refs[-1]
    for at in range(count_in):
        out[at] = refs[at][...]


def join(blocks, after):
    block = blocks[0]
    return pl.pallas_call(
        functools.partial(join_kernel, len(blocks)),
        out_shape=jax.ShapeDtypeStruct((len(blocks), *block.shape), block.dtype),
        in_specs=[vmem_spec()] * len(blocks) + [any_spec()] * len(after),
        out_specs=vmem_spec(),
        compiler_params=params(),
        cost_estimate=COST,
        name="join",
    )(*blocks, *after)


def release_kernel(count, *refs):
    for block, out in zip(refs[:count], refs[-count:]):
        out[...] = block[...]


def release(blocks, after):
    return pl.pallas_call(
        functools.partial(release_kernel, len(blocks)),
        out_shape=[jax.ShapeDtypeStruct(block.shape, block.dtype) for block in blocks],
        in_specs=[vmem_spec()] * len(blocks) + [any_spec()] * len(after),
        out_specs=[vmem_spec()] * len(blocks),
        compiler_params=params(),
        cost_estimate=PACE,
        name="release",
    )(*blocks, *after)


def product_kernel(k, n, planes, me_ref, wave_ref, fold_row_ref, fold_col_ref, *refs):
    near_ref, far_ref, core_ref = refs[:3]
    outs, raw_ref, full_ref = refs[-planes - 2 : -2], refs[-2], refs[-1]
    me = me_ref[0]
    shots, points = near_ref.shape[3:]

    def rows_of(j, i):
        start = ((PLANE * j + i) ^ me) * shots
        return pl.ds(pl.multiple_of(start, shots), shots)

    def block(j, i, b, c):
        if i % 2:
            return core_ref[i // 2, j, b, c]
        return (far_ref if i // 2 else near_ref)[j, b, c]

    s = lax.broadcasted_iota(jnp.int32, (points, points), 0)
    x = lax.broadcasted_iota(jnp.int32, (points, points), 1)
    apart = jnp.abs(x - s)
    recorded = apart < fold_col_ref[...]
    mirrored = apart < fold_row_ref[...]

    def dot(left, right):
        return jnp.dot(left, right, preferred_element_type=jnp.float32)

    half = planes * shots
    for b in range(PLANE):
        for c in range(2):
            for j in range(planes):
                for i in range(PLANE):
                    raw_ref[b, c, rows_of(j, i), :] = block(j, i, b, c)
            own = raw_ref[b, c].astype(jnp.float32)
            full_ref[b, c] = jnp.where(
                recorded, own, jnp.where(mirrored, own.T, 0.0)
            ).astype(jnp.bfloat16)
        left = jnp.concatenate(
            [full_ref[b, c, rows_of(j, 0), :] for c in range(2) for j in range(planes)],
            axis=0,
        )
        by_re, by_im = dot(left, full_ref[b, 0]), dot(left, full_ref[b, 1])
        prod_re = by_re[:half] - by_im[half:]
        prod_im = by_im[:half] + by_re[half:]
        which = k * n + (me // PLANE) * PLANE + b
        wave_re, wave_im = wave_ref[0, which], wave_ref[1, which]
        made_re = (-(wave_re * prod_re - wave_im * prod_im)).astype(jnp.bfloat16)
        made_im = (-(wave_re * prod_im + wave_im * prod_re)).astype(jnp.bfloat16)
        for j, out in enumerate(outs):
            out[b, 0] = made_re[j * shots : (j + 1) * shots]
            out[b, 1] = made_im[j * shots : (j + 1) * shots]


def product(me, wave, fold, near, far, core, k, n, after):
    planes, _, _, shots, points = near.shape
    block = jax.ShapeDtypeStruct(near.shape[1:], near.dtype)
    return pl.pallas_call(
        functools.partial(product_kernel, k, n, planes),
        out_shape=[block] * planes,
        in_specs=[smem_spec()] * 2 + [vmem_spec()] * 5 + [any_spec()] * len(after),
        out_specs=[vmem_spec()] * planes,
        scratch_shapes=[pltpu.VMEM((PLANE, 2, points, points), jnp.bfloat16)] * 2,
        compiler_params=params(),
        cost_estimate=COST,
        name="product",
    )(me, wave, fold.reshape(1, -1), fold.reshape(-1, 1), near, far, core, *after)


def send(block, n, offset, what):
    with jax.named_scope(what):
        return lax.ppermute(block, "shot", [(d, d ^ offset) for d in range(n)])


def chunked_shards(n, spectra, fold_counts, inverse_wavelet):
    bins = spectra.shape[2]
    chunks, planes = bins // n, n // PLANE
    cross = list(reversed(range(planes // 2, planes)))
    rest = list(range(1, planes // 2))
    me = lax.axis_index("shot").astype(jnp.int32).reshape(1)

    last = []
    crossed = []

    def order():
        return last[-1:] + crossed[-2:-1]

    def depart(blocks, what):
        for j, block in blocks.items():
            if j:
                blocks[j] = send(block, n, PLANE * j, f"{what}_z{j}")
            if j in cross:
                crossed.append(blocks[j])
        return blocks

    arrived = [{} for _ in range(chunks)]
    beside = [{} for _ in range(chunks)]
    made = [{} for _ in range(chunks)]
    leaving = [{} for _ in range(chunks)]
    result, merge = [None], []

    def parts(at):
        return [cross[at]] + (([0] + rest) if at == len(cross) - 1 else [])

    def go_in(k, at):
        if k >= chunks:
            return
        wanted = parts(at)
        with jax.named_scope(f"in{k}_{at}"):
            own, at_chunk = spectra, k
            if k == 0 and at == 0:
                blocks = [first(me, spectra, wanted[0])]
            else:
                blocks = relayout(me, own, at_chunk, n, wanted, order())
        last.append(blocks[0])
        arrived[k].update(depart(dict(zip(wanted, blocks)), f"in{k}"))

    def go_out(k, at):
        if not 0 <= k < chunks:
            return
        wanted = parts(at)
        with jax.named_scope(f"out{k}_{at}"):
            blocks = release([made[k][j] for j in wanted], order())
        last.append(blocks[0])
        leaving[k].update(depart(dict(zip(wanted, blocks)), f"out{k}"))

    def go_y(k):
        if not 0 <= k < chunks:
            return
        with jax.named_scope(f"y{k}"):
            near = join([arrived[k][j] for j in range(planes)], last[-1:])
        last.append(near)
        beside[k] = near, send(near, n, 2, f"in{k}_y")

    def go_core(k):
        if not 0 <= k < chunks:
            return
        with jax.named_scope(f"core{k}"):
            both = join(beside[k], last[-1:])
        last.append(both)
        beside[k] += (send(both, n, 1, f"in{k}_core"),)

    def multiply(k):
        if not 0 <= k < chunks:
            return
        with jax.named_scope(f"chunk{k}"):
            blocks = product(
                me, inverse_wavelet, fold_counts, *beside[k], k, n, last[-1:]
            )
        last.append(blocks[0])
        made[k] = dict(enumerate(blocks))

    begun = {}

    def begin_finish(k):
        if not 0 <= k < chunks:
            return
        blocks = {j: leaving[k][j] for j in range(planes) if j != cross[-1]}
        with jax.named_scope(f"chunk{k}"):
            begun[k] = early(
                merge[0], blocks, last[-1:], PACE if k == chunks - 2 else COST
            )
        last.append(begun[k])

    def finish(k):
        if not 0 <= k < chunks:
            return
        blocks = {cross[-1]: leaving[k][cross[-1]]}
        with jax.named_scope(f"chunk{k}"):
            result[0] = assemble(merge[0], begun[k], blocks, result[0], k, n, bins, [])

    for t in range(chunks):
        for at in range(len(cross)):
            go_in(t, at)
            if at == 0:
                multiply(t - 3)
        go_core(t - 2)
        if t == 1:
            merge.append(merge_order(me, n, spectra.shape[0], last[-1:]))
            last.append(merge[0])
        go_y(t - 1)
    for t in range(chunks):
        go_out(t, 0)
        if t == 0:
            multiply(chunks - 3)
        else:
            go_core(chunks - 3 + t)
            go_y(chunks - 2 + t)
        go_out(t, 1)
        if t:
            multiply(chunks - 3 + t)
        begin_finish(t - 1)
        finish(t - 1)
    begin_finish(chunks - 1)
    finish(chunks - 1)
    return result[0]


def solution(mesh):
    n = mesh.shape["shot"]

    def shards(spectra, fold_counts, inverse_wavelet):
        shots, _, bins, _ = spectra.shape
        if n == 4 * PLANE and bins % n == 0 and bins // n >= 4 and shots % 16 == 0:
            return chunked_shards(n, spectra, fold_counts, inverse_wavelet)
        return plain_shards(spectra, fold_counts, inverse_wavelet)

    in_specs = (P(("groups", "shot"), None, None, None), P("groups"), P())
    out_specs = P(("groups", "shot"), None, None, None)
    return jax.shard_map(
        shards, mesh=mesh, in_specs=in_specs, out_specs=out_specs, check_vma=False
    )
```

```python
import functools

import jax
import jax.numpy as jnp
from jax import lax
from jax.experimental import pallas as pl
from jax.experimental.pallas import tpu as pltpu
from jax.sharding import PartitionSpec as P

PLANE = 4
VMEM_LIMIT = 32 * 1024 * 1024


def batched_product(left_operand, right_operand):
    return jnp.einsum(
        "hwi,iwc->hwc", left_operand, right_operand, preferred_element_type=jnp.float32
    )


def plain_shards(spectra, fold_counts, inverse_wavelet):
    points = spectra.shape[3]
    everyone = jnp.arange(points, dtype=jnp.int32)
    regrouped = lax.all_to_all(spectra, "shot", split_axis=2, concat_axis=0, tiled=True)
    recorded = jnp.abs(everyone[None, :] - everyone[:, None]) < fold_counts[:, None]
    flipped = regrouped.transpose(3, 1, 2, 0)
    regrouped = jnp.where(
        recorded[:, None, None, :],
        regrouped,
        jnp.where(recorded.T[:, None, None, :], flipped, jnp.zeros_like(regrouped)),
    )
    local_bins = regrouped.shape[2]
    real_component = regrouped[:, 0]
    imaginary_component = regrouped[:, 1]
    prod_real = batched_product(real_component, real_component) - batched_product(
        imaginary_component, imaginary_component
    )
    prod_imag = batched_product(real_component, imaginary_component) + batched_product(
        imaginary_component, real_component
    )
    first_bin = lax.axis_index("shot") * local_bins
    wave = lax.dynamic_slice_in_dim(inverse_wavelet, first_bin, local_bins, 1)
    wavelet_real = wave[0][None, :, None]
    wave_imag = wave[1][None, :, None]
    output_real = -(wavelet_real * prod_real - wave_imag * prod_imag)
    out_imag = -(wavelet_real * prod_imag + wave_imag * prod_real)
    result = jnp.stack([output_real, out_imag], axis=1).astype(jnp.bfloat16)
    return lax.all_to_all(result, "shot", split_axis=0, concat_axis=2, tiled=True)


def any_spec():
    return pl.BlockSpec(memory_space=pl.ANY)


def vmem_spec():
    return pl.BlockSpec(memory_space=pltpu.VMEM)


def hbm_spec():
    return pl.BlockSpec(memory_space=pltpu.HBM)


def smem_spec():
    return pl.BlockSpec(memory_space=pltpu.SMEM)


def params():
    return pltpu.CompilerParams(vmem_limit_bytes=VMEM_LIMIT)


COST = pl.CostEstimate(flops=0, bytes_accessed=0, transcendentals=0)
PACE = pl.CostEstimate(flops=40_000_000_000, bytes_accessed=0, transcendentals=0)


def split_order(me, n, shots, wanted):
    rows, count = n * shots, PLANE * shots
    source = lax.broadcasted_iota(jnp.int32, (count, rows), 1)
    target = lax.broadcasted_iota(jnp.int32, (count, rows), 0)
    parts = []
    for j in wanted:
        which = ((me // PLANE) ^ j) * PLANE + target // shots
        parts.append((target % shots) * n + which == source)
    return jnp.concatenate(
        [jnp.where(part, 1.0, 0.0).astype(jnp.bfloat16) for part in parts], axis=0
    )


def merge_order_kernel(n, shots, me_ref, *refs):
    out = refs[-1]
    planes, rows, count = out.shape
    source = lax.broadcasted_iota(jnp.int32, (rows, count), 1)
    target = lax.broadcasted_iota(jnp.int32, (rows, count), 0)
    for j in range(planes):
        first = ((me_ref[0] // PLANE) ^ j) * PLANE
        hit = (target % n - first) * shots + target // n == source
        out[j] = jnp.where(hit, 1.0, 0.0).astype(jnp.bfloat16)


def merge_order(me, n, shots, after):
    return pl.pallas_call(
        functools.partial(merge_order_kernel, n, shots),
        out_shape=jax.ShapeDtypeStruct(
            (n // PLANE, n * shots, PLANE * shots), jnp.bfloat16
        ),
        in_specs=[smem_spec()] + [any_spec()] * len(after),
        out_specs=vmem_spec(),
        compiler_params=params(),
        cost_estimate=COST,
        name="merge_order",
    )(me, *after)


def merged(order_ref, blocks, c):
    total = None
    for j, block in blocks:
        rows = block[:, c].reshape(-1, block.shape[3])
        part = jnp.dot(order_ref[j], rows, preferred_element_type=jnp.float32)
        total = part if total is None else total + part
    return total


def early_kernel(which, order_ref, *refs):
    ins, out = refs[: len(which)], refs[-1]
    for c in range(2):
        out[c] = merged(order_ref, list(zip(which, ins)), c).astype(jnp.bfloat16)


def early(order, blocks, after, cost):
    _, _, shots, points = next(iter(blocks.values())).shape
    return pl.pallas_call(
        functools.partial(early_kernel, list(blocks)),
        out_shape=jax.ShapeDtypeStruct((2, order.shape[1], points), jnp.bfloat16),
        in_specs=[vmem_spec()] * (1 + len(blocks)) + [any_spec()] * len(after),
        out_specs=vmem_spec(),
        compiler_params=params(),
        cost_estimate=cost,
        name="early",
    )(order, *blocks.values(), *after)


PIECES = 2


def assemble_kernel(n, shots, k, which, order_ref, begun_ref, *refs):
    ins = refs[: len(which)]
    out, held, sems = refs[-3:]
    copies = []
    part = shots // PIECES
    for c in range(2):
        for p in range(PIECES):
            rows = pl.ds(p * part * n, part * n)
            total = begun_ref[c, rows, :].astype(jnp.float32)
            for j, block in zip(which, ins):
                total = total + jnp.dot(
                    order_ref[j, rows, :],
                    block[:, c].reshape(-1, block.shape[3]),
                    preferred_element_type=jnp.float32,
                )
            at = pl.ds(p * part, part)
            held[c, at] = total.astype(jnp.bfloat16).reshape(part, n, -1)
            copies.append(
                pltpu.make_async_copy(
                    held.at[c, at],
                    out.at[at, c, pl.ds(k * n, n), :],
                    sems.at[len(copies)],
                )
            )
            copies[-1].start()
    for copy in copies:
        copy.wait()


def assemble(order, begun, blocks, result, k, n, bins, after):
    _, _, shots, points = next(iter(blocks.values())).shape
    extra = [] if result is None else [result]
    return pl.pallas_call(
        functools.partial(assemble_kernel, n, shots, k, list(blocks)),
        out_shape=jax.ShapeDtypeStruct((shots, 2, bins, points), jnp.bfloat16),
        in_specs=[vmem_spec()] * (2 + len(blocks))
        + [hbm_spec()] * len(extra)
        + [any_spec()] * len(after),
        out_specs=hbm_spec(),
        scratch_shapes=[
            pltpu.VMEM((2, shots, n, points), jnp.bfloat16),
            pltpu.SemaphoreType.DMA((2 * PIECES,)),
        ],
        input_output_aliases={2 + len(blocks): 0} if extra else {},
        compiler_params=params(),
        cost_estimate=COST,
        name="assemble",
    )(order, begun, *blocks.values(), *extra, *after)


def relayout_kernel(n, shots, wanted, me_ref, x_ref, *refs):
    outs = refs[-len(wanted) :]
    me = me_ref[0]
    order = split_order(me, n, shots, wanted)
    points = x_ref.shape[3]
    for c in range(2):
        rows = x_ref[:, c].reshape(shots * n, points)
        moved = jnp.dot(order, rows, preferred_element_type=jnp.float32)
        moved = moved.astype(jnp.bfloat16).reshape(-1, PLANE, shots, points)
        for at, out in enumerate(outs):
            out[:, c] = moved[at]


def relayout(me, spectra, k, n, wanted, after):
    shots, _, _, points = spectra.shape
    block = jax.ShapeDtypeStruct((PLANE, 2, shots, points), spectra.dtype)
    return pl.pallas_call(
        functools.partial(relayout_kernel, n, shots, wanted),
        grid=(1,),
        out_shape=[block] * len(wanted),
        in_specs=[
            smem_spec(),
            pl.BlockSpec((shots, 2, n, points), lambda _: (0, 0, k, 0)),
        ]
        + [any_spec()] * len(after),
        out_specs=[pl.BlockSpec(block.shape, lambda _: (0, 0, 0, 0))] * len(wanted),
        compiler_params=params(),
        cost_estimate=PACE,
        name="relayout",
    )(me, spectra, *after)


def first_kernel(shots, wanted, me_ref, x_ref, out):
    width, points = x_ref.shape[2:]
    rows, count = shots * width, PLANE * shots
    source = lax.broadcasted_iota(jnp.int32, (count, rows), 1)
    target = lax.broadcasted_iota(jnp.int32, (count, rows), 0)
    plane = (me_ref[0] // PLANE) ^ wanted
    bins = (plane * PLANE) % width + target // shots
    hit = (target % shots) * width + bins == source
    order = jnp.where(hit, 1.0, 0.0).astype(jnp.bfloat16)
    for c in range(2):
        block = x_ref[:, c].reshape(rows, points)
        moved = jnp.dot(order, block, preferred_element_type=jnp.float32)
        out[:, c] = moved.astype(jnp.bfloat16).reshape(PLANE, shots, points)


def first(me, spectra, wanted):
    shots, _, _, points = spectra.shape
    width = 2 * PLANE
    start = (((me[0] // PLANE) ^ wanted) * PLANE) // width * width
    few = lax.dynamic_slice_in_dim(spectra, start, width, axis=2)
    return pl.pallas_call(
        functools.partial(first_kernel, shots, wanted),
        out_shape=jax.ShapeDtypeStruct((PLANE, 2, shots, points), spectra.dtype),
        in_specs=[smem_spec(), vmem_spec()],
        out_specs=vmem_spec(),
        compiler_params=params(),
        cost_estimate=PACE,
        name="first",
    )(me, few)


def join_kernel(count_in, *refs):
    out = refs[-1]
    for at in range(count_in):
        out[at] = refs[at][...]


def join(blocks, after):
    block = blocks[0]
    return pl.pallas_call(
        functools.partial(join_kernel, len(blocks)),
        out_shape=jax.ShapeDtypeStruct((len(blocks), *block.shape), block.dtype),
        in_specs=[vmem_spec()] * len(blocks) + [any_spec()] * len(after),
        out_specs=vmem_spec(),
        compiler_params=params(),
        cost_estimate=COST,
        name="join",
    )(*blocks, *after)


def release_kernel(count, *refs):
    for block, out in zip(refs[:count], refs[-count:]):
        out[...] = block[...]


def release(blocks, after):
    return pl.pallas_call(
        functools.partial(release_kernel, len(blocks)),
        out_shape=[jax.ShapeDtypeStruct(block.shape, block.dtype) for block in blocks],
        in_specs=[vmem_spec()] * len(blocks) + [any_spec()] * len(after),
        out_specs=[vmem_spec()] * len(blocks),
        compiler_params=params(),
        cost_estimate=PACE,
        name="release",
    )(*blocks, *after)


def product_kernel(k, n, planes, me_ref, wave_ref, fold_row_ref, fold_col_ref, *refs):
    near_ref, far_ref, core_ref = refs[:3]
    outs, raw_ref, full_ref = refs[-planes - 2 : -2], refs[-2], refs[-1]
    me = me_ref[0]
    shots, points = near_ref.shape[3:]

    def rows_of(j, i):
        start = ((PLANE * j + i) ^ me) * shots
        return pl.ds(pl.multiple_of(start, shots), shots)

    def block(j, i, b, c):
        if i % 2:
            return core_ref[i // 2, j, b, c]
        return (far_ref if i // 2 else near_ref)[j, b, c]

    s = lax.broadcasted_iota(jnp.int32, (points, points), 0)
    x = lax.broadcasted_iota(jnp.int32, (points, points), 1)
    apart = jnp.abs(x - s)
    recorded = apart < fold_col_ref[...]
    mirrored = apart < fold_row_ref[...]

    def dot(left, right):
        return jnp.dot(left, right, preferred_element_type=jnp.float32)

    half = planes * shots
    for b in range(PLANE):
        for c in range(2):
            for j in range(planes):
                for i in range(PLANE):
                    raw_ref[b, c, rows_of(j, i), :] = block(j, i, b, c)
            own = raw_ref[b, c].astype(jnp.float32)
            full_ref[b, c] = jnp.where(
                recorded, own, jnp.where(mirrored, own.T, 0.0)
            ).astype(jnp.bfloat16)
        left = jnp.concatenate(
            [full_ref[b, c, rows_of(j, 0), :] for c in range(2) for j in range(planes)],
            axis=0,
        )
        by_re, by_im = dot(left, full_ref[b, 0]), dot(left, full_ref[b, 1])
        prod_re = by_re[:half] - by_im[half:]
        prod_im = by_im[:half] + by_re[half:]
        which = k * n + (me // PLANE) * PLANE + b
        wave_re, wave_im = wave_ref[0, which], wave_ref[1, which]
        made_re = (-(wave_re * prod_re - wave_im * prod_im)).astype(jnp.bfloat16)
        made_im = (-(wave_re * prod_im + wave_im * prod_re)).astype(jnp.bfloat16)
        for j, out in enumerate(outs):
            out[b, 0] = made_re[j * shots : (j + 1) * shots]
            out[b, 1] = made_im[j * shots : (j + 1) * shots]


def product(me, wave, fold, near, far, core, k, n, after):
    planes, _, _, shots, points = near.shape
    block = jax.ShapeDtypeStruct(near.shape[1:], near.dtype)
    return pl.pallas_call(
        functools.partial(product_kernel, k, n, planes),
        out_shape=[block] * planes,
        in_specs=[smem_spec()] * 2 + [vmem_spec()] * 5 + [any_spec()] * len(after),
        out_specs=[vmem_spec()] * planes,
        scratch_shapes=[pltpu.VMEM((PLANE, 2, points, points), jnp.bfloat16)] * 2,
        compiler_params=params(),
        cost_estimate=COST,
        name="product",
    )(me, wave, fold.reshape(1, -1), fold.reshape(-1, 1), near, far, core, *after)


def send(block, n, offset, what):
    with jax.named_scope(what):
        return lax.ppermute(block, "shot", [(d, d ^ offset) for d in range(n)])


def chunked_shards(n, spectra, fold_counts, inverse_wavelet):
    bins = spectra.shape[2]
    chunks, planes = bins // n, n // PLANE
    cross = list(reversed(range(planes // 2, planes)))
    rest = list(range(1, planes // 2))
    me = lax.axis_index("shot").astype(jnp.int32).reshape(1)

    last = []
    crossed = []

    def order():
        return last[-1:] + crossed[-2:-1]

    def depart(blocks, what):
        for j, block in blocks.items():
            if j:
                blocks[j] = send(block, n, PLANE * j, f"{what}_z{j}")
            if j in cross:
                crossed.append(blocks[j])
        return blocks

    arrived = [{} for _ in range(chunks)]
    beside = [{} for _ in range(chunks)]
    made = [{} for _ in range(chunks)]
    leaving = [{} for _ in range(chunks)]
    result, merge = [None], []

    def parts(at, over):
        return [over[at]] + (([0] + rest) if at == len(over) - 1 else [])

    def go_in(k, at):
        if k >= chunks:
            return
        wanted = parts(at, cross if k else cross[::-1])
        with jax.named_scope(f"in{k}_{at}"):
            own, at_chunk = spectra, k
            if k == 0 and at == 0:
                blocks = [first(me, spectra, wanted[0])]
            else:
                blocks = relayout(me, own, at_chunk, n, wanted, order())
        last.append(blocks[0])
        arrived[k].update(depart(dict(zip(wanted, blocks)), f"in{k}"))

    def go_out(k, at):
        if not 0 <= k < chunks:
            return
        wanted = parts(at, cross)
        with jax.named_scope(f"out{k}_{at}"):
            blocks = release([made[k][j] for j in wanted], order())
        last.append(blocks[0])
        leaving[k].update(depart(dict(zip(wanted, blocks)), f"out{k}"))

    def go_y(k):
        if not 0 <= k < chunks:
            return
        with jax.named_scope(f"y{k}"):
            near = join([arrived[k][j] for j in range(planes)], last[-1:])
        last.append(near)
        beside[k] = near, send(near, n, 2, f"in{k}_y")

    def go_core(k):
        if not 0 <= k < chunks:
            return
        with jax.named_scope(f"core{k}"):
            both = join(beside[k], last[-1:])
        last.append(both)
        beside[k] += (send(both, n, 1, f"in{k}_core"),)

    def multiply(k):
        if not 0 <= k < chunks:
            return
        with jax.named_scope(f"chunk{k}"):
            blocks = product(
                me, inverse_wavelet, fold_counts, *beside[k], k, n, last[-1:]
            )
        last.append(blocks[0])
        made[k] = dict(enumerate(blocks))

    begun = {}

    def begin_finish(k):
        if not 0 <= k < chunks:
            return
        blocks = {j: leaving[k][j] for j in range(planes) if j != cross[-1]}
        with jax.named_scope(f"chunk{k}"):
            begun[k] = early(
                merge[0], blocks, last[-1:], PACE if k == chunks - 2 else COST
            )
        last.append(begun[k])

    def finish(k):
        if not 0 <= k < chunks:
            return
        blocks = {cross[-1]: leaving[k][cross[-1]]}
        with jax.named_scope(f"chunk{k}"):
            result[0] = assemble(merge[0], begun[k], blocks, result[0], k, n, bins, [])

    for t in range(chunks):
        for at in range(len(cross)):
            go_in(t, at)
            if at == 0:
                multiply(t - 3)
        go_core(t - 2)
        if t == 1:
            merge.append(merge_order(me, n, spectra.shape[0], last[-1:]))
            last.append(merge[0])
        go_y(t - 1)
    for t in range(chunks):
        go_out(t, 0)
        if t == 0:
            multiply(chunks - 3)
        else:
            go_core(chunks - 3 + t)
            go_y(chunks - 2 + t)
        go_out(t, 1)
        if t:
            multiply(chunks - 3 + t)
        begin_finish(t - 1)
        finish(t - 1)
    begin_finish(chunks - 1)
    finish(chunks - 1)
    return result[0]


def solution(mesh):
    n = mesh.shape["shot"]

    def shards(spectra, fold_counts, inverse_wavelet):
        shots, _, bins, _ = spectra.shape
        if n == 4 * PLANE and bins % n == 0 and bins // n >= 4 and shots % 16 == 0:
            return chunked_shards(n, spectra, fold_counts, inverse_wavelet)
        return plain_shards(spectra, fold_counts, inverse_wavelet)

    in_specs = (P(("groups", "shot"), None, None, None), P("groups"), P())
    out_specs = P(("groups", "shot"), None, None, None)
    return jax.shard_map(
        shards, mesh=mesh, in_specs=in_specs, out_specs=out_specs, check_vma=False
    )
```

```python
import functools

import jax
import jax.numpy as jnp
from jax import lax
from jax.experimental import pallas as pl
from jax.experimental.pallas import tpu as pltpu
from jax.sharding import PartitionSpec as P

PLANE = 4
VMEM_LIMIT = 32 * 1024 * 1024


def batched_product(left_operand, right_operand):
    return jnp.einsum(
        "hwi,iwc->hwc", left_operand, right_operand, preferred_element_type=jnp.float32
    )


def plain_shards(spectra, fold_counts, inverse_wavelet):
    points = spectra.shape[3]
    everyone = jnp.arange(points, dtype=jnp.int32)
    regrouped = lax.all_to_all(spectra, "shot", split_axis=2, concat_axis=0, tiled=True)
    recorded = jnp.abs(everyone[None, :] - everyone[:, None]) < fold_counts[:, None]
    flipped = regrouped.transpose(3, 1, 2, 0)
    regrouped = jnp.where(
        recorded[:, None, None, :],
        regrouped,
        jnp.where(recorded.T[:, None, None, :], flipped, jnp.zeros_like(regrouped)),
    )
    local_bins = regrouped.shape[2]
    real_component = regrouped[:, 0]
    imaginary_component = regrouped[:, 1]
    prod_real = batched_product(real_component, real_component) - batched_product(
        imaginary_component, imaginary_component
    )
    prod_imag = batched_product(real_component, imaginary_component) + batched_product(
        imaginary_component, real_component
    )
    first_bin = lax.axis_index("shot") * local_bins
    wave = lax.dynamic_slice_in_dim(inverse_wavelet, first_bin, local_bins, 1)
    wavelet_real = wave[0][None, :, None]
    wave_imag = wave[1][None, :, None]
    output_real = -(wavelet_real * prod_real - wave_imag * prod_imag)
    out_imag = -(wavelet_real * prod_imag + wave_imag * prod_real)
    result = jnp.stack([output_real, out_imag], axis=1).astype(jnp.bfloat16)
    return lax.all_to_all(result, "shot", split_axis=0, concat_axis=2, tiled=True)


def any_spec():
    return pl.BlockSpec(memory_space=pl.ANY)


def vmem_spec():
    return pl.BlockSpec(memory_space=pltpu.VMEM)


def hbm_spec():
    return pl.BlockSpec(memory_space=pltpu.HBM)


def smem_spec():
    return pl.BlockSpec(memory_space=pltpu.SMEM)


def params():
    return pltpu.CompilerParams(vmem_limit_bytes=VMEM_LIMIT)


COST = pl.CostEstimate(flops=0, bytes_accessed=0, transcendentals=0)
PACE = pl.CostEstimate(flops=40_000_000_000, bytes_accessed=0, transcendentals=0)


def split_order(me, n, shots, wanted):
    rows, count = n * shots, PLANE * shots
    source = lax.broadcasted_iota(jnp.int32, (count, rows), 1)
    target = lax.broadcasted_iota(jnp.int32, (count, rows), 0)
    parts = []
    for j in wanted:
        which = ((me // PLANE) ^ j) * PLANE + target // shots
        parts.append((target % shots) * n + which == source)
    return jnp.concatenate(
        [jnp.where(part, 1.0, 0.0).astype(jnp.bfloat16) for part in parts], axis=0
    )


def merge_order_kernel(n, shots, me_ref, *refs):
    out = refs[-1]
    planes, rows, count = out.shape
    source = lax.broadcasted_iota(jnp.int32, (rows, count), 1)
    target = lax.broadcasted_iota(jnp.int32, (rows, count), 0)
    for j in range(planes):
        first = ((me_ref[0] // PLANE) ^ j) * PLANE
        hit = (target % n - first) * shots + target // n == source
        out[j] = jnp.where(hit, 1.0, 0.0).astype(jnp.bfloat16)


def merge_order(me, n, shots, after):
    return pl.pallas_call(
        functools.partial(merge_order_kernel, n, shots),
        out_shape=jax.ShapeDtypeStruct(
            (n // PLANE, n * shots, PLANE * shots), jnp.bfloat16
        ),
        in_specs=[smem_spec()] + [any_spec()] * len(after),
        out_specs=vmem_spec(),
        compiler_params=params(),
        cost_estimate=COST,
        name="merge_order",
    )(me, *after)


def merged(order_ref, blocks, c):
    total = None
    for j, block in blocks:
        rows = block[:, c].reshape(-1, block.shape[3])
        part = jnp.dot(order_ref[j], rows, preferred_element_type=jnp.float32)
        total = part if total is None else total + part
    return total


def early_kernel(which, order_ref, *refs):
    ins, out = refs[: len(which)], refs[-1]
    for c in range(2):
        out[c] = merged(order_ref, list(zip(which, ins)), c).astype(jnp.bfloat16)


def early(order, blocks, after, cost):
    _, _, shots, points = next(iter(blocks.values())).shape
    return pl.pallas_call(
        functools.partial(early_kernel, list(blocks)),
        out_shape=jax.ShapeDtypeStruct((2, order.shape[1], points), jnp.bfloat16),
        in_specs=[vmem_spec()] * (1 + len(blocks)) + [any_spec()] * len(after),
        out_specs=vmem_spec(),
        compiler_params=params(),
        cost_estimate=cost,
        name="early",
    )(order, *blocks.values(), *after)


def assemble_kernel(n, shots, k, which, order_ref, begun_ref, *refs):
    ins = refs[: len(which)]
    out, held, sems = refs[-3:]
    copies = []
    for c in range(2):
        total = merged(order_ref, list(zip(which, ins)), c)
        total = total + begun_ref[c].astype(jnp.float32)
        held[c] = total.astype(jnp.bfloat16).reshape(shots, n, -1)
        copies.append(
            pltpu.make_async_copy(
                held.at[c], out.at[:, c, pl.ds(k * n, n), :], sems.at[c]
            )
        )
        copies[c].start()
    for copy in copies:
        copy.wait()


def assemble(order, begun, blocks, result, k, n, bins, after):
    _, _, shots, points = next(iter(blocks.values())).shape
    extra = [] if result is None else [result]
    return pl.pallas_call(
        functools.partial(assemble_kernel, n, shots, k, list(blocks)),
        out_shape=jax.ShapeDtypeStruct((shots, 2, bins, points), jnp.bfloat16),
        in_specs=[vmem_spec()] * (2 + len(blocks))
        + [hbm_spec()] * len(extra)
        + [any_spec()] * len(after),
        out_specs=hbm_spec(),
        scratch_shapes=[
            pltpu.VMEM((2, shots, n, points), jnp.bfloat16),
            pltpu.SemaphoreType.DMA((2,)),
        ],
        input_output_aliases={2 + len(blocks): 0} if extra else {},
        compiler_params=params(),
        cost_estimate=COST,
        name="assemble",
    )(order, begun, *blocks.values(), *extra, *after)


def relayout_kernel(n, shots, wanted, me_ref, x_ref, *refs):
    outs = refs[-len(wanted) :]
    me = me_ref[0]
    order = split_order(me, n, shots, wanted)
    points = x_ref.shape[3]
    for c in range(2):
        rows = x_ref[:, c].reshape(shots * n, points)
        moved = jnp.dot(order, rows, preferred_element_type=jnp.float32)
        moved = moved.astype(jnp.bfloat16).reshape(-1, PLANE, shots, points)
        for at, out in enumerate(outs):
            out[:, c] = moved[at]


def relayout(me, spectra, k, n, wanted, after):
    shots, _, _, points = spectra.shape
    block = jax.ShapeDtypeStruct((PLANE, 2, shots, points), spectra.dtype)
    return pl.pallas_call(
        functools.partial(relayout_kernel, n, shots, wanted),
        grid=(1,),
        out_shape=[block] * len(wanted),
        in_specs=[
            smem_spec(),
            pl.BlockSpec((shots, 2, n, points), lambda _: (0, 0, k, 0)),
        ]
        + [any_spec()] * len(after),
        out_specs=[pl.BlockSpec(block.shape, lambda _: (0, 0, 0, 0))] * len(wanted),
        compiler_params=params(),
        cost_estimate=PACE,
        name="relayout",
    )(me, spectra, *after)


def first_kernel(shots, wanted, me_ref, x_ref, out):
    width, points = x_ref.shape[2:]
    rows, count = shots * width, PLANE * shots
    source = lax.broadcasted_iota(jnp.int32, (count, rows), 1)
    target = lax.broadcasted_iota(jnp.int32, (count, rows), 0)
    plane = (me_ref[0] // PLANE) ^ wanted
    bins = (plane * PLANE) % width + target // shots
    hit = (target % shots) * width + bins == source
    order = jnp.where(hit, 1.0, 0.0).astype(jnp.bfloat16)
    for c in range(2):
        block = x_ref[:, c].reshape(rows, points)
        moved = jnp.dot(order, block, preferred_element_type=jnp.float32)
        out[:, c] = moved.astype(jnp.bfloat16).reshape(PLANE, shots, points)


def first(me, spectra, wanted):
    shots, _, _, points = spectra.shape
    width = 2 * PLANE
    start = (((me[0] // PLANE) ^ wanted) * PLANE) // width * width
    few = lax.dynamic_slice_in_dim(spectra, start, width, axis=2)
    return pl.pallas_call(
        functools.partial(first_kernel, shots, wanted),
        out_shape=jax.ShapeDtypeStruct((PLANE, 2, shots, points), spectra.dtype),
        in_specs=[smem_spec(), vmem_spec()],
        out_specs=vmem_spec(),
        compiler_params=params(),
        cost_estimate=PACE,
        name="first",
    )(me, few)


def join_kernel(count_in, *refs):
    out = refs[-1]
    for at in range(count_in):
        out[at] = refs[at][...]


def join(blocks, after):
    block = blocks[0]
    return pl.pallas_call(
        functools.partial(join_kernel, len(blocks)),
        out_shape=jax.ShapeDtypeStruct((len(blocks), *block.shape), block.dtype),
        in_specs=[vmem_spec()] * len(blocks) + [any_spec()] * len(after),
        out_specs=vmem_spec(),
        compiler_params=params(),
        cost_estimate=COST,
        name="join",
    )(*blocks, *after)


def release_kernel(count, *refs):
    for block, out in zip(refs[:count], refs[-count:]):
        out[...] = block[...]


def release(blocks, after):
    return pl.pallas_call(
        functools.partial(release_kernel, len(blocks)),
        out_shape=[jax.ShapeDtypeStruct(block.shape, block.dtype) for block in blocks],
        in_specs=[vmem_spec()] * len(blocks) + [any_spec()] * len(after),
        out_specs=[vmem_spec()] * len(blocks),
        compiler_params=params(),
        cost_estimate=PACE,
        name="release",
    )(*blocks, *after)


def product_kernel(k, n, planes, me_ref, wave_ref, fold_row_ref, fold_col_ref, *refs):
    near_ref, far_ref, core_ref = refs[:3]
    outs, raw_ref, full_ref = refs[-planes - 2 : -2], refs[-2], refs[-1]
    me = me_ref[0]
    shots, points = near_ref.shape[3:]

    def rows_of(j, i):
        start = ((PLANE * j + i) ^ me) * shots
        return pl.ds(pl.multiple_of(start, shots), shots)

    def block(j, i, b, c):
        if i % 2:
            return core_ref[i // 2, j, b, c]
        return (far_ref if i // 2 else near_ref)[j, b, c]

    s = lax.broadcasted_iota(jnp.int32, (points, points), 0)
    x = lax.broadcasted_iota(jnp.int32, (points, points), 1)
    apart = jnp.abs(x - s)
    recorded = apart < fold_col_ref[...]
    mirrored = apart < fold_row_ref[...]

    def dot(left, right):
        return jnp.dot(left, right, preferred_element_type=jnp.float32)

    half = planes * shots
    for b in range(PLANE):
        for c in range(2):
            for j in range(planes):
                for i in range(PLANE):
                    raw_ref[b, c, rows_of(j, i), :] = block(j, i, b, c)
            own = raw_ref[b, c].astype(jnp.float32)
            full_ref[b, c] = jnp.where(
                recorded, own, jnp.where(mirrored, own.T, 0.0)
            ).astype(jnp.bfloat16)
        left = jnp.concatenate(
            [full_ref[b, c, rows_of(j, 0), :] for c in range(2) for j in range(planes)],
            axis=0,
        )
        by_re, by_im = dot(left, full_ref[b, 0]), dot(left, full_ref[b, 1])
        prod_re = by_re[:half] - by_im[half:]
        prod_im = by_im[:half] + by_re[half:]
        which = k * n + (me // PLANE) * PLANE + b
        wave_re, wave_im = wave_ref[0, which], wave_ref[1, which]
        made_re = (-(wave_re * prod_re - wave_im * prod_im)).astype(jnp.bfloat16)
        made_im = (-(wave_re * prod_im + wave_im * prod_re)).astype(jnp.bfloat16)
        for j, out in enumerate(outs):
            out[b, 0] = made_re[j * shots : (j + 1) * shots]
            out[b, 1] = made_im[j * shots : (j + 1) * shots]


def product(me, wave, fold, near, far, core, k, n, after):
    planes, _, _, shots, points = near.shape
    block = jax.ShapeDtypeStruct(near.shape[1:], near.dtype)
    return pl.pallas_call(
        functools.partial(product_kernel, k, n, planes),
        out_shape=[block] * planes,
        in_specs=[smem_spec()] * 2 + [vmem_spec()] * 5 + [any_spec()] * len(after),
        out_specs=[vmem_spec()] * planes,
        scratch_shapes=[pltpu.VMEM((PLANE, 2, points, points), jnp.bfloat16)] * 2,
        compiler_params=params(),
        cost_estimate=COST,
        name="product",
    )(me, wave, fold.reshape(1, -1), fold.reshape(-1, 1), near, far, core, *after)


def send(block, n, offset, what):
    with jax.named_scope(what):
        return lax.ppermute(block, "shot", [(d, d ^ offset) for d in range(n)])


def chunked_shards(n, spectra, fold_counts, inverse_wavelet):
    bins = spectra.shape[2]
    chunks, planes = bins // n, n // PLANE
    cross = list(reversed(range(planes // 2, planes)))
    rest = list(range(1, planes // 2))
    me = lax.axis_index("shot").astype(jnp.int32).reshape(1)

    last = []
    crossed = []

    def order():
        return last[-1:] + crossed[-2:-1]

    def depart(blocks, what):
        for j, block in blocks.items():
            if j:
                blocks[j] = send(block, n, PLANE * j, f"{what}_z{j}")
            if j in cross:
                crossed.append(blocks[j])
        return blocks

    arrived = [{} for _ in range(chunks)]
    beside = [{} for _ in range(chunks)]
    made = [{} for _ in range(chunks)]
    leaving = [{} for _ in range(chunks)]
    result, merge = [None], []

    def crossing(k):
        return cross[::-1] if k % 2 == 0 else cross

    def parts(at, over=cross):
        return [over[at]] + (([0] + rest) if at == len(over) - 1 else [])

    def go_in(k, at):
        if k >= chunks:
            return
        wanted = parts(at, cross)
        with jax.named_scope(f"in{k}_{at}"):
            own, at_chunk = spectra, k
            if k == 0 and at == 0:
                blocks = [first(me, spectra, wanted[0])]
            else:
                blocks = relayout(me, own, at_chunk, n, wanted, order())
        last.append(blocks[0])
        arrived[k].update(depart(dict(zip(wanted, blocks)), f"in{k}"))

    def go_out(k, at):
        if not 0 <= k < chunks:
            return
        wanted = parts(at, crossing(k))
        with jax.named_scope(f"out{k}_{at}"):
            blocks = release([made[k][j] for j in wanted], order())
        last.append(blocks[0])
        leaving[k].update(depart(dict(zip(wanted, blocks)), f"out{k}"))

    def go_y(k):
        if not 0 <= k < chunks:
            return
        with jax.named_scope(f"y{k}"):
            near = join([arrived[k][j] for j in range(planes)], last[-1:])
        last.append(near)
        beside[k] = near, send(near, n, 2, f"in{k}_y")

    def go_core(k):
        if not 0 <= k < chunks:
            return
        with jax.named_scope(f"core{k}"):
            both = join(beside[k], last[-1:])
        last.append(both)
        beside[k] += (send(both, n, 1, f"in{k}_core"),)

    def multiply(k):
        if not 0 <= k < chunks:
            return
        with jax.named_scope(f"chunk{k}"):
            blocks = product(
                me, inverse_wavelet, fold_counts, *beside[k], k, n, last[-1:]
            )
        last.append(blocks[0])
        made[k] = dict(enumerate(blocks))

    begun = {}

    def begin_finish(k):
        if not 0 <= k < chunks:
            return
        blocks = {j: leaving[k][j] for j in range(planes) if j != crossing(k)[-1]}
        with jax.named_scope(f"chunk{k}"):
            begun[k] = early(
                merge[0], blocks, last[-1:], PACE if k == chunks - 2 else COST
            )
        last.append(begun[k])

    def finish(k):
        if not 0 <= k < chunks:
            return
        blocks = {crossing(k)[-1]: leaving[k][crossing(k)[-1]]}
        with jax.named_scope(f"chunk{k}"):
            result[0] = assemble(merge[0], begun[k], blocks, result[0], k, n, bins, [])

    for t in range(chunks):
        for at in range(len(cross)):
            go_in(t, at)
            if at == 0:
                multiply(t - 3)
        go_core(t - 2)
        if t == 1:
            merge.append(merge_order(me, n, spectra.shape[0], last[-1:]))
            last.append(merge[0])
        go_y(t - 1)
    for t in range(chunks):
        go_out(t, 0)
        if t == 0:
            multiply(chunks - 3)
        else:
            go_core(chunks - 3 + t)
            go_y(chunks - 2 + t)
        go_out(t, 1)
        if t:
            multiply(chunks - 3 + t)
        begin_finish(t - 1)
        finish(t - 1)
    begin_finish(chunks - 1)
    finish(chunks - 1)
    return result[0]


def solution(mesh):
    n = mesh.shape["shot"]

    def shards(spectra, fold_counts, inverse_wavelet):
        shots, _, bins, _ = spectra.shape
        if n == 4 * PLANE and bins % n == 0 and bins // n >= 4 and shots % 16 == 0:
            return chunked_shards(n, spectra, fold_counts, inverse_wavelet)
        return plain_shards(spectra, fold_counts, inverse_wavelet)

    in_specs = (P(("groups", "shot"), None, None, None), P("groups"), P())
    out_specs = P(("groups", "shot"), None, None, None)
    return jax.shard_map(
        shards, mesh=mesh, in_specs=in_specs, out_specs=out_specs, check_vma=False
    )
```
